32 devices in a mesh: grp: 2 (over x), row: 16 (over z, y, core).
Axes of the slice: x: 2, y: 2, z: 4, core: 2. Of those that a mesh axis runs over, the one named last changes fastest.
Arguments:
- amp_exch: bfloat16 [256, 256, 256], P(('grp', 'row')), parts along dimension 0, may hold values from -250 to 250
- pno_energy: float32 [256, 256], P(('grp', 'row')), parts along dimension 0, may hold values from 0.3 to 3
- pair_gap: float32 [256], P(('grp', 'row')), parts along dimension 0, may hold values from 0.5 to 1.5
- fock: float32 [256, 8], P(('grp', 'row')), parts along dimension 0, may hold values from -0.4 to 0.4
- intersection: bfloat16 [256, 8, 256, 256], P(('grp', 'row')), parts along dimension 0, may hold values from -0.375 to 0.375
- nbr_slot: int32 [256, 8], P(('grp', 'row')), parts along dimension 0, may hold values from 4 to 19, as said below
- nbr_live: int32 [256, 8], P(('grp', 'row')), parts along dimension 0, may hold values from 0 to 1, as said below
- pair_live: int32 [256], P(('grp', 'row')), parts along dimension 0, may hold values 0 or 1
Outputs:
- amplitudes: float32 [256, 256, 256], P(('grp', 'row')), parts along dimension 0
- residual_norms: float32 [4], P('grp'), parts along dimension 0
The draws below stay inside these ranges and needn't reach their ends.
There are 2 independent parts, one for each index of `grp`. The reference program is written for one: setup_inputs(seed, part) draws one part's arguments, and reference() takes and returns one part's arrays. A program takes and returns all parts, laid end to end along the dimension named above; each array names one. Nothing has to cross between parts.
Inputs may be any that keep to these rules, and one draw needn't show every extreme that they name: `nbr_slot`: an entry names a slot among the last 4 of the previous device, any slot of this device, or among the first 4 of the next device; both ends are named in every draw. `nbr_live`: the share of live entries differs from device to device.
All inputs are finite; a program needn't handle non-finite values. No bound on the sum of `pair_live` on one device may be relied on, other than what follows from the above.
Results may differ from the reference program's by a relative error of at most 0.0029.
Values may be sent and summed in bfloat16 or wider, within the bound.
No kernel may reach another device: no remote copies, remote signals or barrier semaphores. Data moves between devices by JAX's collectives and lax.ppermute only.
A program may use at most 64 MiB of HBM per device.

```python
import math
import jax
import jax.numpy as jnp
from jax import lax

V = 256
PAIR_DEV = 8
NB = 8
ITERS = 2
REACH = 4
PAIRS = 128


def draw_amp_exch(key, part):
    key = jax.random.fold_in(key, 11)
    key_noise, key_rows, key_cols = jax.random.split(key, 3)
    position = jnp.arange(PAIRS, dtype=jnp.float32) / max(PAIRS - 1, 1)
    row_scale = jnp.exp(jax.random.uniform(key_rows, (PAIRS, V, 1), jnp.float32, math.log(0.3), math.log(3.0)))
    col_scale = jnp.exp(jax.random.uniform(key_cols, (PAIRS, 1, V), jnp.float32, math.log(0.3), math.log(3.0)))
    noise = jax.random.normal(key_noise, (PAIRS, V, V), jnp.float32)
    growth = 1.0 + 2.0 * position
    return (noise * row_scale * col_scale * growth[:, None, None]).astype(jnp.bfloat16)


def draw_nbr_slot(key, part):
    key = jax.random.fold_in(key, 21)
    drawn = jax.random.randint(key, (PAIRS, NB), 0, 1048576)
    column = jnp.arange(NB, dtype=jnp.int32)[None, :]
    before = PAIR_DEV - REACH + drawn % REACH
    after = 2 * PAIR_DEV + drawn % REACH
    inside = PAIR_DEV + drawn % PAIR_DEV
    slots = jnp.where(column < 2, before, jnp.where(column < 4, after, inside))
    leading = (jnp.arange(PAIRS, dtype=jnp.int32) % PAIR_DEV == 0)[:, None]
    slots = jnp.where(leading & (column == 0), PAIR_DEV - REACH, slots)
    slots = jnp.where(leading & (column == 2), 2 * PAIR_DEV + REACH - 1, slots)
    return slots.astype(jnp.int32)


def draw_nbr_live(key, part):
    key = jax.random.fold_in(key, 31)
    key_budget, key_entry = jax.random.split(key)
    budget = jax.random.randint(key_budget, (PAIRS // PAIR_DEV,), 1, NB + 1)
    device = jnp.arange(PAIRS, dtype=jnp.int32) // PAIR_DEV
    drawn = jax.random.randint(key_entry, (PAIRS, NB), 0, NB)
    return (drawn < budget[device][:, None]).astype(jnp.int32)


def place_ends(result, rng, least, high):
    extent = result.shape
    place = [jax.random.randint(jax.random.fold_in(rng, axis), (), 0, extent[axis]) for axis in range(len(extent))]
    result = result.at[tuple(place)].set(least)
    longest = extent.index(max(extent))
    place[longest] = (place[longest] + 1) % extent[longest]
    return result.at[tuple(place)].set(high)


def shard_levels(rng, extent, cuts, least, top_value):
    loudness = 1.0
    for dim, parts in cuts:
        steps = jax.random.uniform(jax.random.fold_in(jax.random.fold_in(rng, 6), dim), (parts,), jnp.float32, least / len(cuts), top_value / len(cuts))
        loudness = loudness * jnp.repeat(jnp.exp(steps), extent[dim] // parts).reshape((-1,) + (1,) * (len(extent) - 1 - dim))
    return loudness


def normal_values(own_key, shape, spread, limit, cuts=(), kind=jnp.bfloat16):
    values = jax.random.normal(own_key, shape, jnp.float32) * spread
    if len(cuts) > 0:
        values = shard_levels(own_key, shape, cuts, -0.22, 0.18) * values
    return jnp.clip(values, min=-limit, max=limit).astype(kind)


def setup_inputs(seed: int = 0, part: int = 0) -> dict:
    arg_keys = jax.random.split(jax.random.key(seed), 9)
    own_keys = jax.random.split(jax.random.fold_in(arg_keys[8], part), 9)
    return {
        "amp_exch": draw_amp_exch(jax.random.fold_in(jax.random.fold_in(arg_keys[8], part), 71), part),
        "pno_energy": jnp.clip(jnp.exp(math.log(3.0) - 2.3025851 * jax.random.uniform(own_keys[1], (PAIRS, V), jnp.float32) ** shard_levels(own_keys[1], (PAIRS, V), ((0, 16),), -0.2, 0.2)), 0.3, 3.0),
        "pair_gap": jnp.clip(0.5 + 1.0 * jax.random.uniform(own_keys[2], (PAIRS,), jnp.float32) ** shard_levels(own_keys[2], (PAIRS,), ((0, 16),), -0.2, 0.2), 0.5, 1.5),
        "fock": jnp.clip(jax.random.uniform(own_keys[3], (PAIRS, NB), jnp.float32, -0.4, 0.4) * shard_levels(own_keys[3], (PAIRS, NB), ((0, 16),), -0.4, 0.0), -0.4, 0.4),
        "intersection": normal_values(own_keys[4], (PAIRS, NB, V, V), V ** -0.5, 0.375, ((0, 16),)),
        "nbr_slot": draw_nbr_slot(jax.random.fold_in(jax.random.fold_in(arg_keys[8], part), 71), part),
        "nbr_live": draw_nbr_live(jax.random.fold_in(jax.random.fold_in(arg_keys[8], part), 71), part),
        "pair_live": place_ends((jax.random.randint(own_keys[7], (PAIRS,), 0, 8) < 7).astype(jnp.int32), jax.random.fold_in(own_keys[7], 1), 0, 1),
    }


def reference(amp_exch, pno_energy, pair_gap, fock, intersection, nbr_slot, nbr_live, pair_live):
    total_pairs = amp_exch.shape[0]
    denominator = pno_energy[:, :, None] + pno_energy[:, None, :] + pair_gap[:, None, None]
    coupling = fock * nbr_live.astype(jnp.float32)
    live_pairs = pair_live.astype(jnp.float32)[:, None, None]
    exchange = amp_exch.astype(jnp.float32)
    amplitudes = -live_pairs * exchange / denominator
    leading = (jnp.arange(total_pairs, dtype=jnp.int32) // PAIR_DEV * PAIR_DEV).astype(jnp.int32)
    src_index = (leading[:, None] + nbr_slot).astype(jnp.int32)
    results = []
    for sweep in range(ITERS):
        rounded = amplitudes.astype(jnp.bfloat16)
        padded = jnp.pad(rounded, ((PAIR_DEV, PAIR_DEV), (0, 0), (0, 0)))

        def pair_coupling(items):
            matrices, indices, factors = items
            sources = padded[indices].astype(jnp.float32)
            mats = matrices.astype(jnp.float32)
            half_done = jnp.einsum('nab,nbc->nac', mats, sources).astype(jnp.bfloat16)
            transformed = jnp.einsum('nac,ndc->nad', half_done.astype(jnp.float32), mats)
            return lax.optimization_barrier(jnp.sum(factors[:, None, None] * transformed, axis=0))
        coupled = lax.map(pair_coupling, (intersection, src_index, coupling))
        residual = live_pairs * (exchange + denominator * amplitudes - coupled)
        squared = jnp.sum(residual * residual)
        results.append(jnp.sqrt(squared / (total_pairs * V * V)))
        amplitudes = amplitudes - residual / denominator
    return (amplitudes, jnp.stack(results))
```

```python
import functools

import jax
import jax.numpy as jnp
from jax import lax
from jax.experimental import pallas as pl
from jax.experimental.pallas import tpu as pltpu
from jax.sharding import PartitionSpec as P

F32 = jnp.float32
BF16 = jnp.bfloat16
VM = pl.BlockSpec(memory_space=pltpu.VMEM)
SM = pl.BlockSpec(memory_space=pltpu.SMEM)
AN = pl.BlockSpec(memory_space=pl.ANY)
CAP = 72
UNROLL = 4
MIB = 1 << 20


def base_slot():
    return lax.rem(lax.axis_index("row"), 2) * 4


def params(mib, **kw):
    return pltpu.CompilerParams(vmem_limit_bytes=mib * MIB, **kw)


def cost(flops, nbytes):
    return pl.CostEstimate(flops=flops, bytes_accessed=nbytes, transcendentals=0)


def vmem(x):
    return pltpu.with_memory_space_constraint(x, pltpu.VMEM)


def denominators(energy, gap, slots):
    rows = [energy[pl.ds(p, 1), :] for p in slots]
    fill = [jnp.zeros_like(rows[0])] * (8 - len(rows))
    cols = jnp.transpose(jnp.concatenate(rows + fill, axis=0))
    return [cols[:, i : i + 1] + rows[i] + gap[p] for i, p in enumerate(slots)]


def start_tiles(first, exch, energy, gap, live, out, buf, sem):
    base = base_slot()
    slots = [(q + base) & 7 for q in range(first, first + 4)]
    copies = [pltpu.make_async_copy(exch.at[p], buf.at[i], sem.at[i]) for i, p in enumerate(slots)]
    for c in copies:
        c.start()
    dens = denominators(energy, gap, slots)
    for i, p in enumerate(slots):
        copies[i].wait()
        out[i] = (-live[p].astype(F32) * buf[i].astype(F32) / dens[i]).astype(BF16)


def first_kernel(exch, energy, gap, live, out, buf, sem):
    start_tiles(0, exch, energy, gap, live, out, buf, sem)


def second_kernel(exch, energy, gap, live, fock, nslot, nlive, out, lists, coefs, counts, buf, sem):
    start_tiles(4, exch, energy, gap, live, out, buf, sem)
    base = base_slot()
    odd = base != 0

    def entry(i, carry):
        na, nxa, nxb = carry
        q, n = i >> 3, i & 7
        p = (q + base) & 7
        v = nslot[p, n]
        on = (nlive[p, n] != 0) & (live[p] != 0)
        one = jnp.where(on, 1, 0)
        prev, nxt = v < 8, v >= 16
        across = (prev & jnp.logical_not(odd)) | (nxt & odd)
        near = (prev & odd) | (nxt & jnp.logical_not(odd))
        index = jnp.where(prev, v - 4, v - 16)
        src = jnp.where(across, index, jnp.where(near, 8 + index, (v - 8 + base) & 7))
        code = (src << 9) | (q << 6) | (p << 3) | n
        pos = jnp.where(across, jnp.where(q < 4, CAP + nxa, 2 * CAP + nxb), na)
        lists[pos] = code
        coefs[pos] = fock[p, n] * nlive[p, n].astype(F32)
        na = na + jnp.where(across, 0, one)
        nxa = nxa + jnp.where(across & (q < 4), one, 0)
        nxb = nxb + jnp.where(across & (q >= 4), one, 0)
        return na, nxa, nxb

    zero = jnp.int32(0)
    ends = lax.fori_loop(0, 64, entry, (zero, zero, zero))
    for k, e in enumerate(ends):
        counts[k] = e
        for u in range(UNROLL):
            lists[k * CAP + e + u] = 0
            coefs[k * CAP + e + u] = 0.0


def run_list(which, lists, coefs, counts, inter, src, acc):
    off = which * CAP
    chunks = (counts[which] + (UNROLL - 1)) // UNROLL

    def chunk(i, _):
        halves = []
        for u in range(UNROLL):
            code = lists[off + i * UNROLL + u]
            n, p, q, s = code & 7, (code >> 3) & 7, (code >> 6) & 7, code >> 9
            x = inter[p, n]
            h = jnp.dot(x, src[s], preferred_element_type=F32).astype(BF16)
            halves.append((coefs[off + i * UNROLL + u], q, x, h))
        for c, q, x, h in halves:
            t = lax.dot_general(h, x, (((1,), (1,)), ((), ())), preferred_element_type=F32)
            acc[q] = acc[q] - c * t
        return 0

    lax.fori_loop(0, chunks, chunk, 0)


def near_kernel_1(lists, coefs, counts, gap, live, inter, exch, energy, x, i, ih, acc, amps, recip, src):
    base = base_slot()
    slots = [(q + base) & 7 for q in range(8)]
    dens = denominators(energy, gap, slots)
    for q, p in enumerate(slots):
        ex = exch[p].astype(F32)
        a0 = -live[p].astype(F32) * ex / dens[q]
        amps[q] = a0
        recip[q] = 1.0 / dens[q]
        acc[q] = ex + dens[q] * a0
    src[0:4] = x[...]
    src[4:8] = i[...]
    src[8:12] = ih[...]
    run_list(0, lists, coefs, counts, inter, src, acc)


def across_kernel(first, lists, coefs, counts, live, inter, xh, recip, acc_in, amps_in, out, acc, amps):
    del acc_in, amps_in
    base = base_slot()
    run_list(1 if first == 0 else 2, lists, coefs, counts, inter, xh, acc)
    for j in range(4):
        q = first + j
        res = live[(q + base) & 7].astype(F32) * acc[q]
        a1 = amps[q] - res * recip[q]
        amps[q] = a1
        out[j] = a1.astype(BF16)


def squares(res):
    s = jnp.sum((res * res).reshape(32, 8, 256), axis=0)
    return s[:, :128] + s[:, 128:]


def near_kernel_2(lists, coefs, counts, gap, live, inter, exch, energy, x, i, ih, amps, acc_in, acc, sq, src):
    del acc_in
    base = base_slot()
    slots = [(q + base) & 7 for q in range(8)]
    dens = denominators(energy, gap, slots)
    total = jnp.zeros((8, 128), F32)
    for q, p in enumerate(slots):
        total = total + squares(live[p].astype(F32) * acc[q])
        acc[q] = exch[p].astype(F32) + dens[q] * amps[q]
    sq[...] = total
    src[0:4] = x[...]
    src[4:8] = i[...]
    src[8:12] = ih[...]
    run_list(0, lists, coefs, counts, inter, src, acc)


def last_kernel(lists, coefs, counts, live, inter, xh, recip, amps, sq1, acc_in, out, sums, acc, buf, sem):
    del acc_in
    base = base_slot()
    total = jnp.zeros((8, 128), F32)
    copies = []
    for half in range(2):
        run_list(1 + half, lists, coefs, counts, inter, xh, acc)
        for q in range(4 * half, 4 * half + 4):
            p = (q + base) & 7
            res = live[p].astype(F32) * acc[q]
            total = total + squares(res)
            buf[q] = amps[q] - res * recip[q]
            copies.append(pltpu.make_async_copy(buf.at[q], out.at[p], sem.at[q]))
            copies[-1].start()
    first = jnp.sum(sq1[...], axis=0, keepdims=True)
    second = jnp.sum(total, axis=0, keepdims=True)
    row = lax.broadcasted_iota(jnp.int32, (8, 128), 0)
    sums[...] = jnp.where(row == 0, first, jnp.where(row == 1, second, 0.0))
    for c in copies:
        c.wait()


def on_device(amp_exch, pno_energy, pair_gap, fock, intersection, nbr_slot, nbr_live, pair_live):
    count = lax.axis_size("row")
    v = amp_exch.shape[-1]
    tiles4 = pltpu.VMEM((4, v, v), BF16)
    tiles8 = pltpu.VMEM((8, v, v), F32)
    stage = [pltpu.VMEM((4, v, v), BF16), pltpu.SemaphoreType.DMA((4,))]
    same_chip = [(i, i ^ 1) for i in range(count) if (i ^ 1) < count]
    other_chip = [(i, i + 1) for i in range(1, count - 1, 2)]
    other_chip += [(j, i) for i, j in other_chip]

    x0 = pl.pallas_call(
        first_kernel, out_shape=tiles4, in_specs=[AN, VM, SM, SM], out_specs=VM, scratch_shapes=stage,
        compiler_params=params(8), cost_estimate=cost(10**6, 10**6), name="first",
    )(amp_exch, pno_energy, pair_gap, pair_live)
    xh = lax.ppermute(x0, "row", other_chip)
    i0, lists, coefs, counts = pl.pallas_call(
        second_kernel,
        out_shape=[tiles4, pltpu.SMEM((3 * CAP,), jnp.int32), pltpu.SMEM((3 * CAP,), F32), pltpu.SMEM((3,), jnp.int32)],
        in_specs=[AN, VM] + [SM] * 5, out_specs=[VM, SM, SM, SM], scratch_shapes=stage,
        compiler_params=params(8), cost_estimate=cost(10**6, 10**6), name="second",
    )(amp_exch, pno_energy, pair_gap, pair_live, fock, nbr_slot, nbr_live)
    ih = lax.ppermute(i0, "row", same_chip)
    inter, exch = vmem(intersection), vmem(amp_exch)
    meta = (lists, coefs, counts)
    gathered = [pltpu.VMEM((12, v, v), BF16)]
    acc, amps, recip = pl.pallas_call(
        near_kernel_1, out_shape=[tiles8] * 3, in_specs=[SM] * 5 + [VM] * 6, out_specs=[VM] * 3, scratch_shapes=gathered,
        compiler_params=params(16), cost_estimate=cost(3 * 10**9, 10**7), name="near1",
    )(*meta, pair_gap, pair_live, inter, exch, pno_energy, vmem(x0), vmem(i0), vmem(ih))

    def across(first, halo, acc, amps):
        return pl.pallas_call(
            functools.partial(across_kernel, first), out_shape=[tiles4, tiles8, tiles8],
            in_specs=[SM] * 4 + [VM] * 5, out_specs=[VM] * 3, input_output_aliases={7: 1, 8: 2},
            compiler_params=params(8), cost_estimate=cost(10**9, 10**6), name=f"across{first}",
        )(*meta, pair_live, inter, vmem(halo), vmem(recip), vmem(acc), vmem(amps))

    x1, acc, amps = across(0, xh, acc, amps)
    xh1 = lax.ppermute(x1, "row", other_chip)
    i1, acc, amps = across(4, xh, acc, amps)
    ih1 = lax.ppermute(i1, "row", same_chip)
    acc, sq = pl.pallas_call(
        near_kernel_2, out_shape=[tiles8, pltpu.VMEM((8, 128), F32)], in_specs=[SM] * 5 + [VM] * 8, out_specs=[VM] * 2,
        scratch_shapes=gathered, input_output_aliases={12: 0},
        compiler_params=params(16), cost_estimate=cost(3 * 10**9, 10**7), name="near2",
    )(*meta, pair_gap, pair_live, inter, exch, pno_energy, vmem(x1), vmem(i1), vmem(ih1), vmem(amps), vmem(acc))
    out, sums, _ = pl.pallas_call(
        last_kernel, out_shape=[jax.ShapeDtypeStruct((8, v, v), F32), pltpu.VMEM((8, 128), F32), tiles8],
        in_specs=[SM] * 4 + [VM] * 6, out_specs=[AN, VM, VM], input_output_aliases={9: 2},
        scratch_shapes=[pltpu.VMEM((8, v, v), F32), pltpu.SemaphoreType.DMA((8,))],
        compiler_params=params(16), cost_estimate=cost(10**9, 10**6), name="last",
    )(*meta, pair_live, inter, vmem(xh1), vmem(recip), vmem(amps), vmem(sq), vmem(acc))
    step = 1
    while step < count:
        sums = sums + lax.ppermute(sums, "row", [(i, i ^ step) for i in range(count)])
        step *= 2
    norms = jnp.sqrt(jnp.sum(sums[:2], axis=1) / (amp_exch.shape[0] * count * v * v))
    return out, norms


def solution(mesh):
    whole = P(("grp", "row"))
    return jax.shard_map(
        on_device, mesh=mesh, in_specs=(whole,) * 8, out_specs=(whole, P("grp")), check_vma=False
    )
```

```python
import functools

import jax
import jax.numpy as jnp
from jax import lax
from jax.experimental import pallas as pl
from jax.experimental.pallas import tpu as pltpu
from jax.sharding import PartitionSpec as P

F32 = jnp.float32
BF16 = jnp.bfloat16
VM = pl.BlockSpec(memory_space=pltpu.VMEM)
SM = pl.BlockSpec(memory_space=pltpu.SMEM)
AN = pl.BlockSpec(memory_space=pl.ANY)
CAP = 72
NEAR, ACROSS = 8, 4
COUNTS, LIVE = 4 * CAP, 4 * CAP + 4
GAP = 4 * CAP
MIB = 1 << 20


def base_slot():
    return lax.rem(lax.axis_index("row"), 2) * 4


def slots_of(first, end):
    base = base_slot()
    return [(q + base) & 7 for q in range(first, end)]


def params(mib, **kw):
    return pltpu.CompilerParams(vmem_limit_bytes=mib * MIB, **kw)


COST = pl.CostEstimate(flops=1000, bytes_accessed=1000, transcendentals=0)


def vmem(x):
    return pltpu.with_memory_space_constraint(x, pltpu.VMEM)


def hbm(x):
    return pltpu.with_memory_space_constraint(x, pltpu.HBM)


def denominators(energy, gaps, slots):
    rows = [energy[pl.ds(p, 1), :] for p in slots]
    fill = [jnp.zeros_like(rows[0])] * (8 - len(rows))
    cols = jnp.transpose(jnp.concatenate(rows + fill, axis=0))
    return [cols[:, i : i + 1] + rows[i] + gaps[i] for i in range(len(slots))]


def start_all(pairs, sems):
    copies = [pltpu.make_async_copy(a, b, sems.at[i]) for i, (a, b) in enumerate(pairs)]
    for c in copies:
        c.start()
    return copies


def first_kernel(exch, energy, gap, live, out, buf, en, gp, lv, sem, sems):
    slots = slots_of(0, 4)
    small = start_all([(energy, en), (gap, gp), (live, lv)], sems)
    tiles = start_all([(exch.at[p], buf.at[i]) for i, p in enumerate(slots)], sem)
    for c in small:
        c.wait()
    dens = denominators(en, [gp[p] for p in slots], slots)
    for i, p in enumerate(slots):
        tiles[i].wait()
        out[i] = (-lv[p].astype(F32) * buf[i].astype(F32) / dens[i]).astype(BF16)


def second_kernel(
    exch, energy, gap, live, fock, nslot, nlive, inter_hbm, x, out_a, out_b, ex, en, lists, coefs, inter,
    gp, lv, fk, ns, nl, table, ends, sem, sems, slab_sem,
):
    del x
    slots = slots_of(4, 8)
    base = base_slot()
    small = start_all([(energy, en), (gap, gp), (live, lv), (fock, fk), (nslot, ns), (nlive, nl)], sems)
    order = slots + slots_of(0, 4)
    tiles = start_all([(exch.at[p], ex.at[p]) for p in order], sem)
    slabs = start_all([(inter_hbm.at[p], inter.at[p]) for p in range(8)], slab_sem)
    for c in small:
        c.wait()
    dens = denominators(en, [gp[p] for p in slots], slots)
    for i, p in enumerate(slots):
        tiles[i].wait()
        tile = (-lv[p].astype(F32) * ex[p].astype(F32) / dens[i]).astype(BF16)
        if i < 2:
            out_a[i] = tile
        else:
            out_b[i - 2] = tile

    for s in range(4):
        table[4 + s] = jnp.where(base == 0, (s << 9) | 3, ((8 + s) << 9) | 1)
        table[16 + s] = jnp.where(base == 0, ((8 + s) << 9) | 1, (s << 9) | 3)
    for s in range(8):
        table[8 + s] = (((s + base) & 7) << 9) | lv[s]
    for k in range(4):
        ends[k] = k * CAP

    def entry(i, _):
        q, n = i >> 3, i & 7
        p = (q + base) & 7
        what = table[ns[p, n]]
        which = (what & 2) + (q >> 2)
        pos = ends[which]
        lists[pos] = ((what >> 9) << 9) | (q << 6) | (p << 3) | n
        coefs[pos] = fk[p, n]
        ends[which] = pos + (nl[p, n] & lv[p] & what & 1)
        return 0

    lax.fori_loop(0, 64, entry, 0, unroll=4)
    for k in range(4):
        e = ends[k]
        lists[COUNTS + k] = e - k * CAP
        for u in range(NEAR if k < 2 else ACROSS):
            lists[e + u] = 0
            coefs[e + u] = 0.0
    for p in range(8):
        lists[LIVE + p] = lv[p]
        coefs[GAP + p] = gp[p]
    for c in tiles[4:] + slabs:
        c.wait()


def run_list(which, lists, coefs, inter, src, acc):
    unroll = NEAR if which < 2 else ACROSS
    off = which * CAP
    chunks = (lists[COUNTS + which] + (unroll - 1)) // unroll

    def chunk(i, _):
        halves = []
        for u in range(unroll):
            code = lists[off + i * unroll + u]
            n, p, q, s = code & 7, (code >> 3) & 7, (code >> 6) & 7, code >> 9
            x = inter[p, n]
            h = jnp.dot(x, src[s], preferred_element_type=F32).astype(BF16)
            halves.append((coefs[off + i * unroll + u], q, x, h))
        for c, q, x, h in halves:
            t = lax.dot_general(h, x, (((1,), (1,)), ((), ())), preferred_element_type=F32)
            acc[q] = acc[q] - c * t
        return 0

    lax.fori_loop(0, chunks, chunk, 0)


def gather(src, x, ia, ib, iha, ihb):
    src[0:4] = x[...]
    src[4:6] = ia[...]
    src[6:8] = ib[...]
    src[8:10] = iha[...]
    src[10:12] = ihb[...]


def near_kernel_1(lists, coefs, inter, exch, energy, x, ia, ib, iha, ihb, acc, amps, recip, src):
    slots = slots_of(0, 8)
    dens = denominators(energy, [coefs[GAP + p] for p in slots], slots)
    gather(src, x, ia, ib, iha, ihb)
    for q, p in enumerate(slots):
        ex = exch[p].astype(F32)
        a0 = -lists[LIVE + p].astype(F32) * ex / dens[q]
        amps[q] = a0
        recip[q] = 1.0 / dens[q]
        acc[q] = ex + dens[q] * a0
    for half in range(2):
        run_list(half, lists, coefs, inter, src, acc)


def across_kernel(half, lists, coefs, inter, xh, recip, acc_in, amps_in, *outs):
    del acc_in, amps_in
    *out, acc, amps = outs
    run_list(2 + half, lists, coefs, inter, xh, acc)
    for j, p in enumerate(slots_of(4 * half, 4 * half + 4)):
        q = 4 * half + j
        res = lists[LIVE + p].astype(F32) * acc[q]
        a1 = amps[q] - res * recip[q]
        amps[q] = a1
        each = 4 // len(out)
        out[j // each][j % each] = a1.astype(BF16)


def squares(res):
    s = jnp.sum((res * res).reshape(32, 8, 256), axis=0)
    return s[:, :128] + s[:, 128:]


def near_kernel_2(lists, coefs, inter, exch, energy, x, ia, ib, iha, ihb, amps, acc_in, acc, sq, src):
    del acc_in
    slots = slots_of(0, 8)
    dens = denominators(energy, [coefs[GAP + p] for p in slots], slots)
    total = jnp.zeros((8, 128), F32)
    for q, p in enumerate(slots):
        total = total + squares(lists[LIVE + p].astype(F32) * acc[q])
        acc[q] = exch[p].astype(F32) + dens[q] * amps[q]
    sq[...] = total
    gather(src, x, ia, ib, iha, ihb)
    for half in range(2):
        run_list(half, lists, coefs, inter, src, acc)


def last_kernel(lists, coefs, inter, xh, recip, amps, sq1, acc_in, out, sums, acc, buf, sem):
    del acc_in
    total = jnp.zeros((8, 128), F32)
    copies = []
    slots = slots_of(0, 8)
    for half in range(2):
        run_list(2 + half, lists, coefs, inter, xh, acc)
        for q in range(4 * half, 4 * half + 4):
            p = slots[q]
            res = lists[LIVE + p].astype(F32) * acc[q]
            total = total + squares(res)
            buf[q] = amps[q] - res * recip[q]
            copies.append(pltpu.make_async_copy(buf.at[q], out.at[p], sem.at[q]))
            copies[-1].start()
    lane = lax.broadcasted_iota(jnp.int32, sums.shape, 1)
    sums[...] = jnp.where(lane == 0, jnp.sum(sq1[...]), jnp.where(lane == 1, jnp.sum(total), 0.0))
    for c in copies:
        c.wait()


def on_device(amp_exch, pno_energy, pair_gap, fock, intersection, nbr_slot, nbr_live, pair_live):
    count = lax.axis_size("row")
    v = amp_exch.shape[-1]
    tiles4 = pltpu.VMEM((4, v, v), BF16)
    tiles8 = pltpu.VMEM((8, v, v), F32)
    dma = pltpu.SemaphoreType.DMA
    per_pair = [pltpu.SMEM((8,), F32), pltpu.SMEM((8,), jnp.int32)]
    same_chip = [(i, i ^ 1) for i in range(count) if (i ^ 1) < count]
    other_chip = [(i, i + 1) for i in range(1, count - 1, 2)]
    other_chip += [(j, i) for i, j in other_chip]
    big = [hbm(a) for a in (amp_exch, pno_energy, pair_gap, pair_live, fock, nbr_slot, nbr_live)]

    x0 = pl.pallas_call(
        first_kernel, out_shape=tiles4, in_specs=[AN] * 4, out_specs=VM,
        scratch_shapes=[pltpu.VMEM((4, v, v), BF16), pltpu.VMEM((8, v), F32)] + per_pair + [dma((4,)), dma((3,))],
        compiler_params=params(8), cost_estimate=COST, name="first",
    )(*big[:4])
    xh = lax.ppermute(x0, "row", other_chip)
    tiles2 = pltpu.VMEM((2, v, v), BF16)
    i0a, i0b, exch, energy, lists, coefs, inter = pl.pallas_call(
        second_kernel,
        out_shape=[tiles2, tiles2, pltpu.VMEM((8, v, v), BF16), pltpu.VMEM((8, v), F32),
                   pltpu.SMEM((LIVE + 8,), jnp.int32), pltpu.SMEM((GAP + 8,), F32), pltpu.VMEM(intersection.shape, BF16)],
        in_specs=[AN] * 9, out_specs=[VM] * 4 + [SM] * 2 + [VM],
        scratch_shapes=per_pair + [pltpu.SMEM((8, 8), F32)] + [pltpu.SMEM((8, 8), jnp.int32)] * 2
        + [pltpu.SMEM((24,), jnp.int32), pltpu.SMEM((4,), jnp.int32), dma((8,)), dma((6,)), dma((8,))],
        compiler_params=params(8), cost_estimate=COST, name="second",
    )(*big, hbm(intersection), x0)

    def swap(*halves):
        return [vmem(lax.ppermute(h, "row", same_chip)) for h in halves]

    meta = (lists, coefs)
    exch, energy, inter = vmem(exch), vmem(energy), vmem(inter)
    gathered = [pltpu.VMEM((12, v, v), BF16)]
    acc, amps, recip = pl.pallas_call(
        near_kernel_1, out_shape=[tiles8] * 3, in_specs=[SM] * 2 + [VM] * 8, out_specs=[VM] * 3, scratch_shapes=gathered,
        compiler_params=params(8), cost_estimate=COST, name="near1",
    )(*meta, inter, exch, energy, vmem(x0), vmem(i0a), vmem(i0b), *swap(i0a, i0b))

    def across(half, halo, acc, amps):
        shapes = [tiles2, tiles2] if half else [tiles4]
        k = len(shapes)
        return pl.pallas_call(
            functools.partial(across_kernel, half), out_shape=shapes + [tiles8, tiles8],
            in_specs=[SM] * 2 + [VM] * 5, out_specs=[VM] * (k + 2), input_output_aliases={5: k, 6: k + 1},
            compiler_params=params(8), cost_estimate=COST, name=f"across{half}",
        )(*meta, inter, vmem(halo), vmem(recip), vmem(acc), vmem(amps))

    x1, acc, amps = across(0, xh, acc, amps)
    xh1 = lax.ppermute(x1, "row", other_chip)
    i1a, i1b, acc, amps = across(1, xh, acc, amps)
    acc, sq = pl.pallas_call(
        near_kernel_2, out_shape=[tiles8, pltpu.VMEM((8, 128), F32)], in_specs=[SM] * 2 + [VM] * 10, out_specs=[VM] * 2,
        scratch_shapes=gathered, input_output_aliases={11: 0},
        compiler_params=params(8), cost_estimate=COST, name="near2",
    )(*meta, inter, exch, energy, vmem(x1), vmem(i1a), vmem(i1b), *swap(i1a, i1b), vmem(amps), vmem(acc))
    out, sums, _ = pl.pallas_call(
        last_kernel, out_shape=[jax.ShapeDtypeStruct((8, v, v), F32), pltpu.VMEM((count, 128), F32), tiles8],
        in_specs=[SM] * 2 + [VM] * 6, out_specs=[AN, VM, VM], input_output_aliases={7: 2},
        scratch_shapes=[pltpu.VMEM((8, v, v), F32), dma((8,))],
        compiler_params=params(8), cost_estimate=COST, name="last",
    )(*meta, inter, vmem(xh1), vmem(recip), vmem(amps), vmem(sq), vmem(acc))
    sums = lax.all_to_all(sums, "row", 0, 0, tiled=True)
    norms = jnp.sqrt(jnp.sum(sums[:, :2], axis=0) / (amp_exch.shape[0] * count * v * v))
    return out, norms


def solution(mesh):
    whole = P(("grp", "row"))
    return jax.shard_map(
        on_device, mesh=mesh, in_specs=(whole,) * 8, out_specs=(whole, P("grp")), check_vma=False
    )
```

```python
import functools

import jax
import jax.numpy as jnp
from jax import lax
from jax.experimental import pallas as pl
from jax.experimental.pallas import tpu as pltpu
from jax.sharding import PartitionSpec as P

F32 = jnp.float32
BF16 = jnp.bfloat16
VM = pl.BlockSpec(memory_space=pltpu.VMEM)
SM = pl.BlockSpec(memory_space=pltpu.SMEM)
AN = pl.BlockSpec(memory_space=pl.ANY)
CAP = 72
LONG, SHORT = 16, 8
COUNTS, LIVE = 4 * CAP, 4 * CAP + 4
GAP = 4 * CAP
MIB = 1 << 20


def base_slot():
    return lax.rem(lax.axis_index("row"), 2) * 4


def slots_of(first, end):
    base = base_slot()
    return [(q + base) & 7 for q in range(first, end)]


def params(mib, **kw):
    return pltpu.CompilerParams(vmem_limit_bytes=mib * MIB, **kw)


COST = pl.CostEstimate(flops=1000, bytes_accessed=1000, transcendentals=0)


def vmem(x):
    return pltpu.with_memory_space_constraint(x, pltpu.VMEM)


def hbm(x):
    return pltpu.with_memory_space_constraint(x, pltpu.HBM)


def denominators(energy, gaps, slots):
    rows = [energy[pl.ds(p, 1), :] for p in slots]
    fill = [jnp.zeros_like(rows[0])] * (8 - len(rows))
    cols = jnp.transpose(jnp.concatenate(rows + fill, axis=0))
    return [cols[:, i : i + 1] + rows[i] + gaps[i] for i in range(len(slots))]


def start_all(pairs, sems):
    copies = [pltpu.make_async_copy(a, b, sems.at[i]) for i, (a, b) in enumerate(pairs)]
    for c in copies:
        c.start()
    return copies


def first_kernel(exch, energy, gap, live, inter_hbm, out, inter, buf, en, gp, lv, sem, sems, slab_sem):
    slots = slots_of(0, 4)
    small = start_all([(energy, en), (gap, gp), (live, lv)], sems)
    tiles = start_all([(exch.at[p], buf.at[i]) for i, p in enumerate(slots)], sem)
    slabs = start_all([(inter_hbm.at[p], inter.at[p]) for p in slots[:1]], slab_sem)
    for c in small:
        c.wait()
    dens = denominators(en, [gp[p] for p in slots], slots)
    for i, p in enumerate(slots):
        tiles[i].wait()
        out[i] = (-lv[p].astype(F32) * buf[i].astype(F32) / dens[i]).astype(BF16)
    for c in slabs:
        c.wait()


def second_kernel(
    exch, energy, gap, live, fock, nslot, nlive, inter_hbm, x, inter_in, out_a, out_b, ex, en, lists, coefs, inter,
    gp, lv, fk, ns, nl, table, ends, sem, sems, slab_sem,
):
    del x, inter_in
    slots = slots_of(4, 8)
    base = base_slot()
    small = start_all([(energy, en), (gap, gp), (live, lv), (fock, fk), (nslot, ns), (nlive, nl)], sems)
    order = slots + slots_of(0, 4)
    tiles = start_all([(exch.at[p], ex.at[p]) for p in order], sem)
    slabs = start_all([(inter_hbm.at[p], inter.at[p]) for p in order[5:]], slab_sem)
    for c in small:
        c.wait()
    dens = denominators(en, [gp[p] for p in slots], slots)
    for i, p in enumerate(slots):
        tiles[i].wait()
        tile = (-lv[p].astype(F32) * ex[p].astype(F32) / dens[i]).astype(BF16)
        if i < 2:
            out_a[i] = tile
        else:
            out_b[i - 2] = tile

    for s in range(4):
        table[4 + s] = jnp.where(base == 0, (s << 9) | 3, ((8 + s) << 9) | 1)
        table[16 + s] = jnp.where(base == 0, ((8 + s) << 9) | 1, (s << 9) | 3)
    for s in range(8):
        table[8 + s] = (((s + base) & 7) << 9) | lv[s]
    for k in range(4):
        ends[k] = k * CAP

    def entry(i, _):
        q, n = i >> 3, i & 7
        p = (q + base) & 7
        what = table[ns[p, n]]
        which = (what & 2) + (q >> 2)
        pos = ends[which]
        lists[pos] = ((what >> 9) << 9) | (q << 6) | (p << 3) | n
        coefs[pos] = fk[p, n]
        ends[which] = pos + (nl[p, n] & lv[p] & what & 1)
        return 0

    lax.fori_loop(0, 64, entry, 0, unroll=4)
    for k in range(4):
        e = ends[k]
        lists[COUNTS + k] = e - k * CAP
        for u in range(LONG):
            lists[e + u] = base << 3
            coefs[e + u] = 0.0
    for p in range(8):
        lists[LIVE + p] = lv[p]
        coefs[GAP + p] = gp[p]
    for c in tiles[4:] + slabs:
        c.wait()


def run_list(which, lists, coefs, inter, src, acc, steps=(LONG, SHORT)):
    off = which * CAP
    count = lists[COUNTS + which]

    def chunk(at, size):
        for u in range(size):
            code = lists[at + u]
            n, p, q, s = code & 7, (code >> 3) & 7, (code >> 6) & 7, code >> 9
            x = inter[p, n]
            h = jnp.dot(x, src[s], preferred_element_type=F32).astype(BF16)
            t = lax.dot_general(h, x, (((1,), (1,)), ((), ())), preferred_element_type=F32)
            acc[q] = acc[q] - coefs[at + u] * t

    if len(steps) > 1:
        longs = (count + steps[0] - steps[1] - 1) // steps[0]
        lax.fori_loop(0, longs, lambda i, _: chunk(off + i * steps[0], steps[0]) or 0, 0)
        off = off + longs * steps[0]
        count = count - longs * steps[0]
    shorts = jnp.maximum(count + steps[-1] - 1, 0) // steps[-1]
    lax.fori_loop(0, shorts, lambda i, _: chunk(off + i * steps[-1], steps[-1]) or 0, 0)


def gather(src, x, ia, ib, iha, ihb):
    src[0:4] = x[...]
    src[4:6] = ia[...]
    src[6:8] = ib[...]
    src[8:10] = iha[...]
    src[10:12] = ihb[...]


def start_half(half, lists, coefs, exch, energy, acc, amps, recip):
    slots = slots_of(4 * half, 4 * half + 4)
    dens = denominators(energy, [coefs[GAP + p] for p in slots], slots)
    for j, p in enumerate(slots):
        q = 4 * half + j
        ex = exch[p].astype(F32)
        a0 = -lists[LIVE + p].astype(F32) * ex / dens[j]
        amps[q] = a0
        recip[q] = 1.0 / dens[j]
        acc[q] = ex + dens[j] * a0


def update_half(half, lists, acc, amps, recip, out):
    each = 4 // len(out)
    for j, p in enumerate(slots_of(4 * half, 4 * half + 4)):
        q = 4 * half + j
        res = lists[LIVE + p].astype(F32) * acc[q]
        a1 = amps[q] - res * recip[q]
        amps[q] = a1
        out[j // each][j % each] = a1.astype(BF16)


def near_kernel_1(lists, coefs, inter_hbm, exch, energy, x, ia, ib, iha, ihb, inter_in, acc, amps, recip, src, inter, sem):
    del inter_in
    slabs = start_all([(inter_hbm.at[p], inter.at[p]) for p in slots_of(4, 8)], sem)
    gather(src, x, ia, ib, iha, ihb)
    start_half(0, lists, coefs, exch, energy, acc, amps, recip)
    run_list(0, lists, coefs, inter, src, acc)
    for c in slabs:
        c.wait()


def across_kernel(lists, coefs, inter, xh, recip, acc_in, amps_in, out, acc, amps):
    del acc_in, amps_in
    run_list(2, lists, coefs, inter, xh, acc, (SHORT,))
    update_half(0, lists, acc, amps, recip, [out])


def rest_kernel(lists, coefs, inter, exch, energy, src, xh, acc_in, amps_in, recip_in, out_a, out_b, acc, amps, recip):
    del acc_in, amps_in, recip_in
    start_half(1, lists, coefs, exch, energy, acc, amps, recip)
    run_list(1, lists, coefs, inter, src, acc)
    run_list(3, lists, coefs, inter, xh, acc, (SHORT,))
    update_half(1, lists, acc, amps, recip, [out_a, out_b])


def squares(res):
    s = jnp.sum((res * res).reshape(32, 8, 256), axis=0)
    return s[:, :128] + s[:, 128:]


def near_kernel_2(lists, coefs, inter, exch, energy, x, ia, ib, iha, ihb, amps, acc_in, acc, sq, src):
    del acc_in
    slots = slots_of(0, 8)
    dens = denominators(energy, [coefs[GAP + p] for p in slots], slots)
    total = jnp.zeros((8, 128), F32)
    for q, p in enumerate(slots):
        total = total + squares(lists[LIVE + p].astype(F32) * acc[q])
        acc[q] = exch[p].astype(F32) + dens[q] * amps[q]
    sq[...] = total
    gather(src, x, ia, ib, iha, ihb)
    for half in range(2):
        run_list(half, lists, coefs, inter, src, acc)


def last_kernel(lists, coefs, inter, xh, recip, amps, sq1, acc_in, out, sums, acc, buf, sem):
    del acc_in
    total = jnp.zeros((8, 128), F32)
    copies = []
    slots = slots_of(0, 8)
    for half in range(2):
        run_list(2 + half, lists, coefs, inter, xh, acc, (SHORT,))
        for q in range(4 * half, 4 * half + 4):
            p = slots[q]
            res = lists[LIVE + p].astype(F32) * acc[q]
            total = total + squares(res)
            buf[q] = amps[q] - res * recip[q]
            copies.append(pltpu.make_async_copy(buf.at[q], out.at[p], sem.at[q]))
            copies[-1].start()
    lane = lax.broadcasted_iota(jnp.int32, sums.shape, 1)
    sums[...] = jnp.where(lane == 0, jnp.sum(sq1[...]), jnp.where(lane == 1, jnp.sum(total), 0.0))
    for c in copies:
        c.wait()


def on_device(amp_exch, pno_energy, pair_gap, fock, intersection, nbr_slot, nbr_live, pair_live):
    count = lax.axis_size("row")
    v = amp_exch.shape[-1]
    tiles4 = pltpu.VMEM((4, v, v), BF16)
    tiles8 = pltpu.VMEM((8, v, v), F32)
    dma = pltpu.SemaphoreType.DMA
    per_pair = [pltpu.SMEM((8,), F32), pltpu.SMEM((8,), jnp.int32)]
    same_chip = [(i, i ^ 1) for i in range(count) if (i ^ 1) < count]
    other_chip = [(i, i + 1) for i in range(1, count - 1, 2)]
    other_chip += [(j, i) for i, j in other_chip]
    big = [hbm(a) for a in (amp_exch, pno_energy, pair_gap, pair_live, fock, nbr_slot, nbr_live)]

    tiles2 = pltpu.VMEM((2, v, v), BF16)
    slabs = pltpu.VMEM(intersection.shape, BF16)
    intersection = hbm(intersection)
    x0, inter = pl.pallas_call(
        first_kernel, out_shape=[tiles4, slabs], in_specs=[AN] * 5, out_specs=[VM] * 2,
        scratch_shapes=[pltpu.VMEM((4, v, v), BF16), pltpu.VMEM((8, v), F32)] + per_pair + [dma((4,)), dma((3,)), dma((1,))],
        compiler_params=params(8), cost_estimate=COST, name="first",
    )(*big[:4], intersection)
    xh = lax.ppermute(x0, "row", other_chip)
    i0a, i0b, exch, energy, lists, coefs, inter = pl.pallas_call(
        second_kernel,
        out_shape=[tiles2, tiles2, pltpu.VMEM((8, v, v), BF16), pltpu.VMEM((8, v), F32),
                   pltpu.SMEM((LIVE + 8,), jnp.int32), pltpu.SMEM((GAP + 8,), F32), slabs],
        in_specs=[AN] * 9 + [VM], out_specs=[VM] * 4 + [SM] * 2 + [VM], input_output_aliases={9: 6},
        scratch_shapes=per_pair + [pltpu.SMEM((8, 8), F32)] + [pltpu.SMEM((8, 8), jnp.int32)] * 2
        + [pltpu.SMEM((24,), jnp.int32), pltpu.SMEM((4,), jnp.int32), dma((8,)), dma((6,)), dma((3,))],
        compiler_params=params(8), cost_estimate=COST, name="second",
    )(*big, intersection, x0, vmem(inter))

    def swap(*halves):
        return [vmem(lax.ppermute(h, "row", same_chip)) for h in halves]

    meta = (lists, coefs)
    exch, energy = vmem(exch), vmem(energy)
    gathered = pltpu.VMEM((12, v, v), BF16)
    acc, amps, recip, src, inter = pl.pallas_call(
        near_kernel_1, out_shape=[tiles8] * 3 + [gathered, slabs], in_specs=[SM] * 2 + [AN] + [VM] * 8, out_specs=[VM] * 5,
        scratch_shapes=[dma((4,))], input_output_aliases={10: 4},
        compiler_params=params(8), cost_estimate=COST, name="near1",
    )(*meta, intersection, exch, energy, vmem(x0), vmem(i0a), vmem(i0b), *swap(i0a, i0b), vmem(inter))
    inter = vmem(inter)
    x1, acc, amps = pl.pallas_call(
        across_kernel, out_shape=[tiles4, tiles8, tiles8],
        in_specs=[SM] * 2 + [VM] * 5, out_specs=[VM] * 3, input_output_aliases={5: 1, 6: 2},
        compiler_params=params(8), cost_estimate=COST, name="across",
    )(*meta, inter, vmem(xh), vmem(recip), vmem(acc), vmem(amps))
    xh1 = lax.ppermute(x1, "row", other_chip)
    i1a, i1b, acc, amps, recip = pl.pallas_call(
        rest_kernel, out_shape=[tiles2, tiles2] + [tiles8] * 3,
        in_specs=[SM] * 2 + [VM] * 8, out_specs=[VM] * 5, input_output_aliases={7: 2, 8: 3, 9: 4},
        compiler_params=params(8), cost_estimate=COST, name="rest",
    )(*meta, inter, exch, energy, vmem(src), vmem(xh), vmem(acc), vmem(amps), vmem(recip))
    acc, sq = pl.pallas_call(
        near_kernel_2, out_shape=[tiles8, pltpu.VMEM((8, 128), F32)], in_specs=[SM] * 2 + [VM] * 10, out_specs=[VM] * 2,
        scratch_shapes=[gathered], input_output_aliases={11: 0},
        compiler_params=params(8), cost_estimate=COST, name="near2",
    )(*meta, inter, exch, energy, vmem(x1), vmem(i1a), vmem(i1b), *swap(i1a, i1b), vmem(amps), vmem(acc))
    out, sums, _ = pl.pallas_call(
        last_kernel, out_shape=[jax.ShapeDtypeStruct((8, v, v), F32), pltpu.VMEM((count, 128), F32), tiles8],
        in_specs=[SM] * 2 + [VM] * 6, out_specs=[AN, VM, VM], input_output_aliases={7: 2},
        scratch_shapes=[pltpu.VMEM((8, v, v), F32), dma((8,))],
        compiler_params=params(8), cost_estimate=COST, name="last",
    )(*meta, inter, vmem(xh1), vmem(recip), vmem(amps), vmem(sq), vmem(acc))
    sums = lax.all_to_all(sums, "row", 0, 0, tiled=True)
    norms = jnp.sqrt(jnp.sum(sums[:, :2], axis=0) / (amp_exch.shape[0] * count * v * v))
    return out, norms


def solution(mesh):
    whole = P(("grp", "row"))
    return jax.shard_map(
        on_device, mesh=mesh, in_specs=(whole,) * 8, out_specs=(whole, P("grp")), check_vma=False
    )
```

```python
import functools

import jax
import jax.numpy as jnp
from jax import lax
from jax.experimental import pallas as pl
from jax.experimental.pallas import tpu as pltpu
from jax.sharding import PartitionSpec as P

F32 = jnp.float32
BF16 = jnp.bfloat16
VM = pl.BlockSpec(memory_space=pltpu.VMEM)
SM = pl.BlockSpec(memory_space=pltpu.SMEM)
AN = pl.BlockSpec(memory_space=pl.ANY)
CAP = 72
LONG, SHORT = 16, 8
COUNTS, LIVE = 4 * CAP, 4 * CAP + 4
GAP = 4 * CAP
MIB = 1 << 20


def base_slot():
    return lax.rem(lax.axis_index("row"), 2) * 4


def slots_of(first, end):
    base = base_slot()
    return [(q + base) & 7 for q in range(first, end)]


def params(mib, **kw):
    return pltpu.CompilerParams(vmem_limit_bytes=mib * MIB, **kw)


COST = pl.CostEstimate(flops=1000, bytes_accessed=1000, transcendentals=0)


def vmem(x):
    return pltpu.with_memory_space_constraint(x, pltpu.VMEM)


def hbm(x):
    return pltpu.with_memory_space_constraint(x, pltpu.HBM)


def denominators(energy, gaps, slots):
    rows = [energy[pl.ds(p, 1), :] for p in slots]
    fill = [jnp.zeros_like(rows[0])] * (8 - len(rows))
    cols = jnp.transpose(jnp.concatenate(rows + fill, axis=0))
    return [cols[:, i : i + 1] + rows[i] + gaps[i] for i in range(len(slots))]


def start_all(pairs, sems):
    copies = [pltpu.make_async_copy(a, b, sems.at[i]) for i, (a, b) in enumerate(pairs)]
    for c in copies:
        c.start()
    return copies


def first_kernel(exch, energy, gap, live, out, buf, en, gp, lv, sem, sems):
    slots = slots_of(0, 4)
    small = start_all([(energy, en), (gap, gp), (live, lv)], sems)
    tiles = start_all([(exch.at[p], buf.at[i]) for i, p in enumerate(slots)], sem)
    for c in small:
        c.wait()
    dens = denominators(en, [gp[p] for p in slots], slots)
    for i, p in enumerate(slots):
        tiles[i].wait()
        out[i] = (-lv[p].astype(F32) * buf[i].astype(F32) / dens[i]).astype(BF16)


def second_kernel(
    exch, energy, gap, live, fock, nslot, nlive, inter_hbm, x, out_a, out_b, ex, en, lists, coefs, inter,
    gp, lv, fk, ns, nl, table, ends, sem, sems, slab_sem,
):
    del x
    slots = slots_of(4, 8)
    base = base_slot()
    small = start_all([(energy, en), (gap, gp), (live, lv), (fock, fk), (nslot, ns), (nlive, nl)], sems)
    order = slots + slots_of(0, 4)
    tiles = start_all([(exch.at[p], ex.at[p]) for p in order], sem)
    slabs = start_all([(inter_hbm.at[p], inter.at[p]) for p in order[4:]], slab_sem)
    for c in small:
        c.wait()
    dens = denominators(en, [gp[p] for p in slots], slots)
    for i, p in enumerate(slots):
        tiles[i].wait()
        tile = (-lv[p].astype(F32) * ex[p].astype(F32) / dens[i]).astype(BF16)
        if i < 2:
            out_a[i] = tile
        else:
            out_b[i - 2] = tile

    for s in range(4):
        table[4 + s] = jnp.where(base == 0, (s << 9) | 3, ((8 + s) << 9) | 1)
        table[16 + s] = jnp.where(base == 0, ((8 + s) << 9) | 1, (s << 9) | 3)
    for s in range(8):
        table[8 + s] = (((s + base) & 7) << 9) | lv[s]
    for k in range(4):
        ends[k] = k * CAP

    def entry(i, _):
        q, n = i >> 3, i & 7
        p = (q + base) & 7
        what = table[ns[p, n]]
        which = (what & 2) + (q >> 2)
        pos = ends[which]
        lists[pos] = ((what >> 9) << 9) | (q << 6) | (p << 3) | n
        coefs[pos] = fk[p, n]
        ends[which] = pos + (nl[p, n] & lv[p] & what & 1)
        return 0

    lax.fori_loop(0, 64, entry, 0, unroll=4)
    for k in range(4):
        e = ends[k]
        lists[COUNTS + k] = e - k * CAP
        for u in range(LONG):
            lists[e + u] = base << 3
            coefs[e + u] = 0.0
    for p in range(8):
        lists[LIVE + p] = lv[p]
        coefs[GAP + p] = gp[p]
    for c in tiles[4:] + slabs:
        c.wait()


def step(at, size, lists, coefs, inter, src, acc):
    for u in range(size):
        code = lists[at + u]
        n, p, q, s = code & 7, (code >> 3) & 7, (code >> 6) & 7, code >> 9
        x = inter[p, n]
        h = jnp.dot(x, src[s], preferred_element_type=F32).astype(BF16)
        t = lax.dot_general(h, x, (((1,), (1,)), ((), ())), preferred_element_type=F32)
        acc[q] = acc[q] - coefs[at + u] * t


def steps(at, count, size, *refs):
    def body(i, _):
        step(at + i * size, size, *refs)
        return 0

    lax.fori_loop(0, count, body, 0)


def near_list(which, lists, *refs):
    at, count = which * CAP, lists[COUNTS + which]
    longs = (count + LONG - SHORT - 1) // LONG
    steps(at, longs, LONG, lists, *refs)
    left = jnp.maximum(count - longs * LONG + SHORT - 1, 0)
    steps(at + longs * LONG, left // SHORT, SHORT, lists, *refs)


def across_list_tail(which, lists, *refs):
    more = jnp.maximum(lists[COUNTS + which] - 1, 0) // SHORT
    steps(which * CAP + SHORT, more, SHORT, lists, *refs)


def gather(src, x, ia, ib, iha, ihb):
    src[0:4] = x[...]
    src[4:6] = ia[...]
    src[6:8] = ib[...]
    src[8:10] = iha[...]
    src[10:12] = ihb[...]


def start_half(half, lists, coefs, exch, energy, acc, amps, recip):
    slots = slots_of(4 * half, 4 * half + 4)
    dens = denominators(energy, [coefs[GAP + p] for p in slots], slots)
    for j, p in enumerate(slots):
        q = 4 * half + j
        ex = exch[p].astype(F32)
        a0 = -lists[LIVE + p].astype(F32) * ex / dens[j]
        amps[q] = a0
        recip[q] = 1.0 / dens[j]
        acc[q] = ex + dens[j] * a0


def update_half(half, lists, acc, amps, recip, out):
    each = 4 // len(out)
    for j, p in enumerate(slots_of(4 * half, 4 * half + 4)):
        q = 4 * half + j
        res = lists[LIVE + p].astype(F32) * acc[q]
        a1 = amps[q] - res * recip[q]
        amps[q] = a1
        out[j // each][j % each] = a1.astype(BF16)


def waits_longer():
    return ((lax.axis_index("row") + 1) & 2) != 0


def near_kernel_1(lists, coefs, inter_hbm, exch, energy, x, ia, ib, iha, ihb, inter_in, acc, amps, recip, src, inter, sem):
    del inter_in
    slabs = start_all([(inter_hbm.at[p], inter.at[p]) for p in slots_of(4, 8)], sem)
    gather(src, x, ia, ib, iha, ihb)
    start_half(0, lists, coefs, exch, energy, acc, amps, recip)
    near_list(0, lists, coefs, inter, src, acc)
    for c in slabs:
        c.wait()

    @pl.when(waits_longer())
    def _():
        start_half(1, lists, coefs, exch, energy, acc, amps, recip)
        near_list(1, lists, coefs, inter, src, acc)


def across_kernel(lists, coefs, inter, xh, recip, acc_in, amps_in, out, acc, amps):
    del acc_in, amps_in
    refs = (lists, coefs, inter, xh, acc)
    across_list_tail(2, *refs)
    step(2 * CAP, SHORT, *refs)
    update_half(0, lists, acc, amps, recip, [out])


def rest_kernel(lists, coefs, inter, exch, energy, src, xh, acc_in, amps_in, recip_in, out_a, out_b, acc, amps, recip):
    del acc_in, amps_in, recip_in

    @pl.when(jnp.logical_not(waits_longer()))
    def _():
        start_half(1, lists, coefs, exch, energy, acc, amps, recip)
        near_list(1, lists, coefs, inter, src, acc)

    refs = (lists, coefs, inter, xh, acc)
    across_list_tail(3, *refs)
    step(3 * CAP, SHORT, *refs)
    update_half(1, lists, acc, amps, recip, [out_a, out_b])


def squares(res):
    s = jnp.sum((res * res).reshape(32, 8, 256), axis=0)
    return s[:, :128] + s[:, 128:]


def near_kernel_2(lists, coefs, inter, exch, energy, x, ia, ib, iha, ihb, amps, acc_in, acc, sq, src):
    del acc_in
    slots = slots_of(0, 8)
    dens = denominators(energy, [coefs[GAP + p] for p in slots], slots)
    total = jnp.zeros((8, 128), F32)
    for q, p in enumerate(slots):
        total = total + squares(lists[LIVE + p].astype(F32) * acc[q])
        acc[q] = exch[p].astype(F32) + dens[q] * amps[q]
    sq[...] = total
    gather(src, x, ia, ib, iha, ihb)
    for half in range(2):
        near_list(half, lists, coefs, inter, src, acc)


def last_kernel(lists, coefs, inter, xh, recip, amps, sq1, acc_in, out, sums, acc, buf, sem):
    del acc_in
    total = jnp.zeros((8, 128), F32)
    copies = []
    slots = slots_of(0, 8)
    refs = (lists, coefs, inter, xh, acc)
    for half in range(2):
        across_list_tail(2 + half, *refs)
    for half in range(2):
        step((2 + half) * CAP, SHORT, *refs)
        for q in range(4 * half, 4 * half + 4):
            p = slots[q]
            res = lists[LIVE + p].astype(F32) * acc[q]
            total = total + squares(res)
            buf[q] = amps[q] - res * recip[q]
            copies.append(pltpu.make_async_copy(buf.at[q], out.at[p], sem.at[q]))
            copies[-1].start()
    rows = (sums.shape[0], 128)
    sums[:, :128] = jnp.broadcast_to(jnp.sum(sq1[...], axis=0, keepdims=True), rows)
    sums[:, 128:] = jnp.broadcast_to(jnp.sum(total, axis=0, keepdims=True), rows)
    for c in copies:
        c.wait()


def on_device(amp_exch, pno_energy, pair_gap, fock, intersection, nbr_slot, nbr_live, pair_live):
    count = lax.axis_size("row")
    v = amp_exch.shape[-1]
    tiles4 = pltpu.VMEM((4, v, v), BF16)
    tiles8 = pltpu.VMEM((8, v, v), F32)
    dma = pltpu.SemaphoreType.DMA
    per_pair = [pltpu.SMEM((8,), F32), pltpu.SMEM((8,), jnp.int32)]
    same_chip = [(i, i ^ 1) for i in range(count) if (i ^ 1) < count]
    other_chip = [(i, i + 1) for i in range(1, count - 1, 2)]
    other_chip += [(j, i) for i, j in other_chip]
    big = [hbm(a) for a in (amp_exch, pno_energy, pair_gap, pair_live, fock, nbr_slot, nbr_live)]

    tiles2 = pltpu.VMEM((2, v, v), BF16)
    slabs = pltpu.VMEM(intersection.shape, BF16)
    intersection = hbm(intersection)
    x0 = pl.pallas_call(
        first_kernel, out_shape=tiles4, in_specs=[AN] * 4, out_specs=VM,
        scratch_shapes=[pltpu.VMEM((4, v, v), BF16), pltpu.VMEM((8, v), F32)] + per_pair + [dma((4,)), dma((3,))],
        compiler_params=params(8), cost_estimate=COST, name="first",
    )(*big[:4])
    xh = lax.ppermute(x0, "row", other_chip)
    i0a, i0b, exch, energy, lists, coefs, inter = pl.pallas_call(
        second_kernel,
        out_shape=[tiles2, tiles2, pltpu.VMEM((8, v, v), BF16), pltpu.VMEM((8, v), F32),
                   pltpu.SMEM((LIVE + 8,), jnp.int32), pltpu.SMEM((GAP + 8,), F32), slabs],
        in_specs=[AN] * 9, out_specs=[VM] * 4 + [SM] * 2 + [VM],
        scratch_shapes=per_pair + [pltpu.SMEM((8, 8), F32)] + [pltpu.SMEM((8, 8), jnp.int32)] * 2
        + [pltpu.SMEM((24,), jnp.int32), pltpu.SMEM((4,), jnp.int32), dma((8,)), dma((6,)), dma((4,))],
        compiler_params=params(8), cost_estimate=COST, name="second",
    )(*big, intersection, x0)

    def swap(*halves):
        return [vmem(lax.ppermute(h, "row", same_chip)) for h in halves]

    meta = (lists, coefs)
    exch, energy = vmem(exch), vmem(energy)
    gathered = pltpu.VMEM((12, v, v), BF16)
    acc, amps, recip, src, inter = pl.pallas_call(
        near_kernel_1, out_shape=[tiles8] * 3 + [gathered, slabs], in_specs=[SM] * 2 + [AN] + [VM] * 8, out_specs=[VM] * 5,
        scratch_shapes=[dma((4,))], input_output_aliases={10: 4},
        compiler_params=params(8), cost_estimate=COST, name="near1",
    )(*meta, intersection, exch, energy, vmem(x0), vmem(i0a), vmem(i0b), *swap(i0a, i0b), vmem(inter))
    inter = vmem(inter)
    x1, acc, amps = pl.pallas_call(
        across_kernel, out_shape=[tiles4, tiles8, tiles8],
        in_specs=[SM] * 2 + [VM] * 5, out_specs=[VM] * 3, input_output_aliases={5: 1, 6: 2},
        compiler_params=params(8), cost_estimate=COST, name="across",
    )(*meta, inter, vmem(xh), vmem(recip), vmem(acc), vmem(amps))
    xh1 = lax.ppermute(x1, "row", other_chip)
    i1a, i1b, acc, amps, recip = pl.pallas_call(
        rest_kernel, out_shape=[tiles2, tiles2] + [tiles8] * 3,
        in_specs=[SM] * 2 + [VM] * 8, out_specs=[VM] * 5, input_output_aliases={7: 2, 8: 3, 9: 4},
        compiler_params=params(8), cost_estimate=COST, name="rest",
    )(*meta, inter, exch, energy, vmem(src), vmem(xh), vmem(acc), vmem(amps), vmem(recip))
    acc, sq = pl.pallas_call(
        near_kernel_2, out_shape=[tiles8, pltpu.VMEM((8, 128), F32)], in_specs=[SM] * 2 + [VM] * 10, out_specs=[VM] * 2,
        scratch_shapes=[gathered], input_output_aliases={11: 0},
        compiler_params=params(8), cost_estimate=COST, name="near2",
    )(*meta, inter, exch, energy, vmem(x1), vmem(i1a), vmem(i1b), *swap(i1a, i1b), vmem(amps), vmem(acc))
    out, sums, _ = pl.pallas_call(
        last_kernel, out_shape=[jax.ShapeDtypeStruct((8, v, v), F32), pltpu.VMEM((count, 256), F32), tiles8],
        in_specs=[SM] * 2 + [VM] * 6, out_specs=[AN, VM, VM], input_output_aliases={7: 2},
        scratch_shapes=[pltpu.VMEM((8, v, v), F32), dma((8,))],
        compiler_params=params(8), cost_estimate=COST, name="last",
    )(*meta, inter, vmem(xh1), vmem(recip), vmem(amps), vmem(sq), vmem(acc))
    sums = lax.all_to_all(sums, "row", 0, 0, tiled=True)
    norms = jnp.sqrt(jnp.sum(sums.reshape(count, 2, 128), axis=(0, 2)) / (amp_exch.shape[0] * count * v * v))
    return out, norms


def solution(mesh):
    whole = P(("grp", "row"))
    return jax.shard_map(
        on_device, mesh=mesh, in_specs=(whole,) * 8, out_specs=(whole, P("grp")), check_vma=False
    )
```

```python
import functools

import jax
import jax.numpy as jnp
from jax import lax
from jax.experimental import pallas as pl
from jax.experimental.pallas import tpu as pltpu
from jax.sharding import PartitionSpec as P

F32 = jnp.float32
BF16 = jnp.bfloat16
VM = pl.BlockSpec(memory_space=pltpu.VMEM)
SM = pl.BlockSpec(memory_space=pltpu.SMEM)
AN = pl.BlockSpec(memory_space=pl.ANY)
CAP = 72
LONG, SHORT = 16, 8
COUNTS, LIVE = 4 * CAP, 4 * CAP + 4
GAP = 4 * CAP
MIB = 1 << 20


def base_slot():
    return lax.rem(lax.axis_index("row"), 2) * 4


def slots_of(first, end):
    base = base_slot()
    return [(q + base) & 7 for q in range(first, end)]


def params(mib, **kw):
    return pltpu.CompilerParams(vmem_limit_bytes=mib * MIB, **kw)


COST = pl.CostEstimate(flops=1000, bytes_accessed=1000, transcendentals=0)


def vmem(x):
    return pltpu.with_memory_space_constraint(x, pltpu.VMEM)


def hbm(x):
    return pltpu.with_memory_space_constraint(x, pltpu.HBM)


def denominators(energy, gaps, slots):
    rows = [energy[pl.ds(p, 1), :] for p in slots]
    fill = [jnp.zeros_like(rows[0])] * (8 - len(rows))
    cols = jnp.transpose(jnp.concatenate(rows + fill, axis=0))
    return [cols[:, i : i + 1] + rows[i] + gaps[i] for i in range(len(slots))]


def start_all(pairs, sems):
    copies = [pltpu.make_async_copy(a, b, sems.at[i]) for i, (a, b) in enumerate(pairs)]
    for c in copies:
        c.start()
    return copies


def goes_second():
    return ((lax.axis_index("row") + 1) & 2) == 0


def prepare_copies(exch, energy, gap, live, fock, nslot, nlive, inter_hbm, ex, en, inter, gp, lv, fk, ns, nl, sem, sems, slab_sem):
    small = [(energy, en), (gap, gp), (live, lv), (fock, fk), (nslot, ns), (nlive, nl)]
    order = slots_of(4, 8) + slots_of(0, 4)
    pairs = [(a, b, sems.at[i]) for i, (a, b) in enumerate(small)]
    pairs += [(exch.at[p], ex.at[p], sem.at[i]) for i, p in enumerate(order)]
    pairs += [(inter_hbm.at[p], inter.at[p], slab_sem.at[i]) for i, p in enumerate(order[4:])]
    return [pltpu.make_async_copy(*three) for three in pairs]


def prepare(copies, out_a, out_b, ex, en, lists, coefs, gp, lv, fk, ns, nl, table, ends):
    slots = slots_of(4, 8)
    base = base_slot()
    for c in copies[:6]:
        c.wait()
    dens = denominators(en, [gp[p] for p in slots], slots)
    for i, p in enumerate(slots):
        copies[6 + i].wait()
        tile = (-lv[p].astype(F32) * ex[p].astype(F32) / dens[i]).astype(BF16)
        if i < 2:
            out_a[i] = tile
        else:
            out_b[i - 2] = tile

    for s in range(4):
        table[4 + s] = jnp.where(base == 0, (s << 9) | 3, ((8 + s) << 9) | 1)
        table[16 + s] = jnp.where(base == 0, ((8 + s) << 9) | 1, (s << 9) | 3)
    for s in range(8):
        table[8 + s] = (((s + base) & 7) << 9) | lv[s]
    for k in range(4):
        ends[k] = k * CAP

    def entry(i, _):
        q, n = i >> 3, i & 7
        p = (q + base) & 7
        what = table[ns[p, n]]
        which = (what & 2) + (q >> 2)
        pos = ends[which]
        lists[pos] = ((what >> 9) << 9) | (q << 6) | (p << 3) | n
        coefs[pos] = fk[p, n]
        ends[which] = pos + (nl[p, n] & lv[p] & what & 1)
        return 0

    lax.fori_loop(0, 64, entry, 0, unroll=4)
    for k in range(4):
        e = ends[k]
        lists[COUNTS + k] = e - k * CAP
        for u in range(LONG):
            lists[e + u] = base << 3
            coefs[e + u] = 0.0
    for p in range(8):
        lists[LIVE + p] = lv[p]
        coefs[GAP + p] = gp[p]
    for c in copies[10:]:
        c.wait()


def first_kernel(*refs):
    ins, (out, out_a, out_b, ex, en, lists, coefs, inter), own, rest = refs[:8], refs[8:16], refs[16:22], refs[22:]
    exch, energy, gap, live = ins[:4]
    buf, en4, gp4, lv4, sem4, sems4 = own
    scalars, sems = rest[:7], rest[7:]
    late = goes_second()
    slots = slots_of(0, 4)
    small = start_all([(energy, en4), (gap, gp4), (live, lv4)], sems4)
    tiles = start_all([(exch.at[p], buf.at[i]) for i, p in enumerate(slots)], sem4)
    copies = prepare_copies(*ins, ex, en, inter, *scalars[:5], *sems)

    @pl.when(late)
    def _():
        for c in copies:
            c.start()

    for c in small:
        c.wait()
    dens = denominators(en4, [gp4[p] for p in slots], slots)
    for i, p in enumerate(slots):
        tiles[i].wait()
        out[i] = (-lv4[p].astype(F32) * buf[i].astype(F32) / dens[i]).astype(BF16)

    @pl.when(late)
    def _():
        prepare(copies, out_a, out_b, ex, en, lists, coefs, *scalars)


def second_kernel(*refs):
    ins, (out_a, out_b, ex, en, lists, coefs, inter), rest = refs[:8], refs[15:22], refs[22:]
    scalars, sems = rest[:7], rest[7:]

    @pl.when(jnp.logical_not(goes_second()))
    def _():
        copies = prepare_copies(*ins, ex, en, inter, *scalars[:5], *sems)
        for c in copies:
            c.start()
        prepare(copies, out_a, out_b, ex, en, lists, coefs, *scalars)


def step(at, size, lists, coefs, inter, src, acc):
    for u in range(size):
        code = lists[at + u]
        n, p, q, s = code & 7, (code >> 3) & 7, (code >> 6) & 7, code >> 9
        x = inter[p, n]
        h = jnp.dot(x, src[s], preferred_element_type=F32).astype(BF16)
        t = lax.dot_general(h, x, (((1,), (1,)), ((), ())), preferred_element_type=F32)
        acc[q] = acc[q] - coefs[at + u] * t


def steps(at, count, size, *refs):
    def body(i, _):
        step(at + i * size, size, *refs)
        return 0

    lax.fori_loop(0, count, body, 0)


def near_list(which, lists, *refs):
    at, count = which * CAP, lists[COUNTS + which]
    longs = (count + LONG - SHORT - 1) // LONG
    steps(at, longs, LONG, lists, *refs)
    left = jnp.maximum(count - longs * LONG + SHORT - 1, 0)
    steps(at + longs * LONG, left // SHORT, SHORT, lists, *refs)


def across_list_tail(which, lists, *refs):
    more = jnp.maximum(lists[COUNTS + which] - 1, 0) // SHORT
    steps(which * CAP + SHORT, more, SHORT, lists, *refs)


def gather(src, x, ia, ib, iha, ihb):
    src[0:4] = x[...]
    src[4:6] = ia[...]
    src[6:8] = ib[...]
    src[8:10] = iha[...]
    src[10:12] = ihb[...]


def start_half(half, lists, coefs, exch, energy, acc, amps, recip):
    slots = slots_of(4 * half, 4 * half + 4)
    dens = denominators(energy, [coefs[GAP + p] for p in slots], slots)
    for j, p in enumerate(slots):
        q = 4 * half + j
        ex = exch[p].astype(F32)
        a0 = -lists[LIVE + p].astype(F32) * ex / dens[j]
        amps[q] = a0
        recip[q] = 1.0 / dens[j]
        acc[q] = ex + dens[j] * a0


def update_half(half, lists, acc, amps, recip, out):
    each = 4 // len(out)
    for j, p in enumerate(slots_of(4 * half, 4 * half + 4)):
        q = 4 * half + j
        res = lists[LIVE + p].astype(F32) * acc[q]
        a1 = amps[q] - res * recip[q]
        amps[q] = a1
        out[j // each][j % each] = a1.astype(BF16)


def near_kernel_1(lists, coefs, inter_hbm, exch, energy, x, ia, ib, iha, ihb, inter_in, acc, amps, recip, src, inter, sem):
    del inter_in
    slabs = start_all([(inter_hbm.at[p], inter.at[p]) for p in slots_of(4, 8)], sem)
    gather(src, x, ia, ib, iha, ihb)
    start_half(0, lists, coefs, exch, energy, acc, amps, recip)
    near_list(0, lists, coefs, inter, src, acc)
    for c in slabs:
        c.wait()

    @pl.when(goes_second())
    def _():
        start_half(1, lists, coefs, exch, energy, acc, amps, recip)
        near_list(1, lists, coefs, inter, src, acc)


def across_kernel(lists, coefs, inter, xh, recip, acc_in, amps_in, out, acc, amps):
    del acc_in, amps_in
    refs = (lists, coefs, inter, xh, acc)
    across_list_tail(2, *refs)
    step(2 * CAP, SHORT, *refs)
    update_half(0, lists, acc, amps, recip, [out])


def rest_kernel(lists, coefs, inter, exch, energy, src, xh, acc_in, amps_in, recip_in, out_a, out_b, acc, amps, recip):
    del acc_in, amps_in, recip_in

    @pl.when(jnp.logical_not(goes_second()))
    def _():
        start_half(1, lists, coefs, exch, energy, acc, amps, recip)
        near_list(1, lists, coefs, inter, src, acc)

    refs = (lists, coefs, inter, xh, acc)
    across_list_tail(3, *refs)
    step(3 * CAP, SHORT, *refs)
    update_half(1, lists, acc, amps, recip, [out_a, out_b])


def squares(res):
    s = jnp.sum((res * res).reshape(32, 8, 256), axis=0)
    return s[:, :128] + s[:, 128:]


def near_kernel_2(lists, coefs, inter, exch, energy, x, ia, ib, iha, ihb, amps, acc_in, acc, sq, src):
    del acc_in
    slots = slots_of(0, 8)
    dens = denominators(energy, [coefs[GAP + p] for p in slots], slots)
    total = jnp.zeros((8, 128), F32)
    for q, p in enumerate(slots):
        total = total + squares(lists[LIVE + p].astype(F32) * acc[q])
        acc[q] = exch[p].astype(F32) + dens[q] * amps[q]
    sq[...] = total
    gather(src, x, ia, ib, iha, ihb)
    for half in range(2):
        near_list(half, lists, coefs, inter, src, acc)


def last_kernel(lists, coefs, inter, xh, recip, amps, sq1, acc_in, out, sums, acc, buf, sem):
    del acc_in
    total = jnp.zeros((8, 128), F32)
    copies = []
    slots = slots_of(0, 8)
    refs = (lists, coefs, inter, xh, acc)
    for half in range(2):
        across_list_tail(2 + half, *refs)
    for half in range(2):
        step((2 + half) * CAP, SHORT, *refs)
        for q in range(4 * half, 4 * half + 4):
            p = slots[q]
            res = lists[LIVE + p].astype(F32) * acc[q]
            total = total + squares(res)
            buf[q] = amps[q] - res * recip[q]
            copies.append(pltpu.make_async_copy(buf.at[q], out.at[p], sem.at[q]))
            copies[-1].start()
    rows = (sums.shape[0], 128)
    sums[:, :128] = jnp.broadcast_to(jnp.sum(sq1[...], axis=0, keepdims=True), rows)
    sums[:, 128:] = jnp.broadcast_to(jnp.sum(total, axis=0, keepdims=True), rows)
    for c in copies:
        c.wait()


def on_device(amp_exch, pno_energy, pair_gap, fock, intersection, nbr_slot, nbr_live, pair_live):
    count = lax.axis_size("row")
    v = amp_exch.shape[-1]
    tiles4 = pltpu.VMEM((4, v, v), BF16)
    tiles8 = pltpu.VMEM((8, v, v), F32)
    dma = pltpu.SemaphoreType.DMA
    per_pair = [pltpu.SMEM((8,), F32), pltpu.SMEM((8,), jnp.int32)]
    same_chip = [(i, i ^ 1) for i in range(count) if (i ^ 1) < count]
    other_chip = [(i, i + 1) for i in range(1, count - 1, 2)]
    other_chip += [(j, i) for i, j in other_chip]
    big = [hbm(a) for a in (amp_exch, pno_energy, pair_gap, pair_live, fock, nbr_slot, nbr_live)]

    tiles2 = pltpu.VMEM((2, v, v), BF16)
    slabs = pltpu.VMEM(intersection.shape, BF16)
    intersection = hbm(intersection)
    shapes = [tiles2, tiles2, pltpu.VMEM((8, v, v), BF16), pltpu.VMEM((8, v), F32),
              pltpu.SMEM((LIVE + 8,), jnp.int32), pltpu.SMEM((GAP + 8,), F32), slabs]
    places = [VM] * 4 + [SM] * 2 + [VM]
    scratch = per_pair + [pltpu.SMEM((8, 8), F32)] + [pltpu.SMEM((8, 8), jnp.int32)] * 2
    scratch += [pltpu.SMEM((24,), jnp.int32), pltpu.SMEM((4,), jnp.int32), dma((8,)), dma((6,)), dma((4,))]
    x0, *made = pl.pallas_call(
        first_kernel, out_shape=[tiles4] + shapes, in_specs=[AN] * 8, out_specs=[VM] + places,
        scratch_shapes=[pltpu.VMEM((4, v, v), BF16), pltpu.VMEM((8, v), F32)] + per_pair + [dma((4,)), dma((3,))] + scratch,
        compiler_params=params(8), cost_estimate=COST, name="first",
    )(*big, intersection)
    xh = lax.ppermute(x0, "row", other_chip)
    made = [m if i in (4, 5) else vmem(m) for i, m in enumerate(made)]
    i0a, i0b, exch, energy, lists, coefs, inter = pl.pallas_call(
        second_kernel, out_shape=shapes, in_specs=[AN] * 8 + places,
        out_specs=places, input_output_aliases={8 + i: i for i in range(7)}, scratch_shapes=scratch,
        compiler_params=params(8), cost_estimate=COST, name="second",
    )(*big, intersection, *made)

    def swap(*halves):
        return [vmem(lax.ppermute(h, "row", same_chip)) for h in halves]

    meta = (lists, coefs)
    exch, energy = vmem(exch), vmem(energy)
    gathered = pltpu.VMEM((12, v, v), BF16)
    acc, amps, recip, src, inter = pl.pallas_call(
        near_kernel_1, out_shape=[tiles8] * 3 + [gathered, slabs], in_specs=[SM] * 2 + [AN] + [VM] * 8, out_specs=[VM] * 5,
        scratch_shapes=[dma((4,))], input_output_aliases={10: 4},
        compiler_params=params(8), cost_estimate=COST, name="near1",
    )(*meta, intersection, exch, energy, vmem(x0), vmem(i0a), vmem(i0b), *swap(i0a, i0b), vmem(inter))
    inter = vmem(inter)
    x1, acc, amps = pl.pallas_call(
        across_kernel, out_shape=[tiles4, tiles8, tiles8],
        in_specs=[SM] * 2 + [VM] * 5, out_specs=[VM] * 3, input_output_aliases={5: 1, 6: 2},
        compiler_params=params(8), cost_estimate=COST, name="across",
    )(*meta, inter, vmem(xh), vmem(recip), vmem(acc), vmem(amps))
    xh1 = lax.ppermute(x1, "row", other_chip)
    i1a, i1b, acc, amps, recip = pl.pallas_call(
        rest_kernel, out_shape=[tiles2, tiles2] + [tiles8] * 3,
        in_specs=[SM] * 2 + [VM] * 8, out_specs=[VM] * 5, input_output_aliases={7: 2, 8: 3, 9: 4},
        compiler_params=params(8), cost_estimate=COST, name="rest",
    )(*meta, inter, exch, energy, vmem(src), vmem(xh), vmem(acc), vmem(amps), vmem(recip))
    acc, sq = pl.pallas_call(
        near_kernel_2, out_shape=[tiles8, pltpu.VMEM((8, 128), F32)], in_specs=[SM] * 2 + [VM] * 10, out_specs=[VM] * 2,
        scratch_shapes=[gathered], input_output_aliases={11: 0},
        compiler_params=params(8), cost_estimate=COST, name="near2",
    )(*meta, inter, exch, energy, vmem(x1), vmem(i1a), vmem(i1b), *swap(i1a, i1b), vmem(amps), vmem(acc))
    out, sums, _ = pl.pallas_call(
        last_kernel, out_shape=[jax.ShapeDtypeStruct((8, v, v), F32), pltpu.VMEM((count, 256), F32), tiles8],
        in_specs=[SM] * 2 + [VM] * 6, out_specs=[AN, VM, VM], input_output_aliases={7: 2},
        scratch_shapes=[pltpu.VMEM((8, v, v), F32), dma((8,))],
        compiler_params=params(8), cost_estimate=COST, name="last",
    )(*meta, inter, vmem(xh1), vmem(recip), vmem(amps), vmem(sq), vmem(acc))
    sums = lax.all_to_all(sums, "row", 0, 0, tiled=True)
    norms = jnp.sqrt(jnp.sum(sums.reshape(count, 2, 128), axis=(0, 2)) / (amp_exch.shape[0] * count * v * v))
    return out, norms


def solution(mesh):
    whole = P(("grp", "row"))
    return jax.shard_map(
        on_device, mesh=mesh, in_specs=(whole,) * 8, out_specs=(whole, P("grp")), check_vma=False
    )
```

```python
import functools

import jax
import jax.numpy as jnp
from jax import lax
from jax.experimental import pallas as pl
from jax.experimental.pallas import tpu as pltpu
from jax.sharding import PartitionSpec as P

F32 = jnp.float32
BF16 = jnp.bfloat16
VM = pl.BlockSpec(memory_space=pltpu.VMEM)
SM = pl.BlockSpec(memory_space=pltpu.SMEM)
AN = pl.BlockSpec(memory_space=pl.ANY)
CAP = 80
LONG, SHORT = 16, 8
LISTS = 7
COUNTS, LIVE = LISTS * CAP, LISTS * CAP + LISTS
GAP = LISTS * CAP
EARLY = 3
MIB = 1 << 20


def base_slot():
    return lax.rem(lax.axis_index("row"), 2) * 4


def slots_of(first, end):
    base = base_slot()
    return [(q + base) & 7 for q in range(first, end)]


def params(mib, **kw):
    return pltpu.CompilerParams(vmem_limit_bytes=mib * MIB, **kw)


COST = pl.CostEstimate(flops=1000, bytes_accessed=1000, transcendentals=0)


def vmem(x):
    return pltpu.with_memory_space_constraint(x, pltpu.VMEM)


def hbm(x):
    return pltpu.with_memory_space_constraint(x, pltpu.HBM)


def denominators(energy, gaps, slots):
    rows = [energy[pl.ds(p, 1), :] for p in slots]
    fill = [jnp.zeros_like(rows[0])] * (8 - len(rows))
    cols = jnp.transpose(jnp.concatenate(rows + fill, axis=0))
    return [cols[:, i : i + 1] + rows[i] + gaps[i] for i in range(len(slots))]


def start_all(pairs, sems):
    copies = [pltpu.make_async_copy(a, b, sems.at[i]) for i, (a, b) in enumerate(pairs)]
    for c in copies:
        c.start()
    return copies


def first_kernel(exch, energy, gap, live, out, buf, en, gp, lv, sem, sems):
    slots = slots_of(0, 4)
    small = start_all([(energy, en), (gap, gp), (live, lv)], sems)
    tiles = start_all([(exch.at[p], buf.at[i]) for i, p in enumerate(slots)], sem)
    for c in small:
        c.wait()
    dens = denominators(en, [gp[p] for p in slots], slots)
    for i, p in enumerate(slots):
        tiles[i].wait()
        out[i] = (-lv[p].astype(F32) * buf[i].astype(F32) / dens[i]).astype(BF16)


def second_kernel(
    exch, energy, gap, live, fock, nslot, nlive, inter_hbm, x, out_a, out_b, ex, en, lists, coefs, inter,
    gp, lv, fk, ns, nl, table, ends, sem, sems, slab_sem,
):
    del x
    slots = slots_of(4, 8)
    base = base_slot()
    small = start_all([(energy, en), (gap, gp), (live, lv), (fock, fk), (nslot, ns), (nlive, nl)], sems)
    order = slots + slots_of(0, 4)
    tiles = start_all([(exch.at[p], ex.at[p]) for p in order], sem)
    slabs = start_all([(inter_hbm.at[p], inter.at[p]) for p in order[4:]], slab_sem)
    for c in small:
        c.wait()
    dens = denominators(en, [gp[p] for p in slots], slots)
    for i, p in enumerate(slots):
        tiles[i].wait()
        tile = (-lv[p].astype(F32) * ex[p].astype(F32) / dens[i]).astype(BF16)
        if i < 2:
            out_a[i] = tile
        else:
            out_b[i - 2] = tile

    for s in range(4):
        table[4 + s] = jnp.where(base == 0, (s << 9) | 3, ((8 + s) << 9) | 1)
        table[16 + s] = jnp.where(base == 0, ((8 + s) << 9) | 1, (s << 9) | 3)
    for s in range(8):
        table[8 + s] = (((s + base) & 7) << 9) | lv[s]
    for k in range(LISTS):
        ends[k] = k * CAP

    def entry(i, _):
        q, n = i >> 3, i & 7
        p = (q + base) & 7
        what = table[ns[p, n]]
        which = (what & 2) + (q >> 2)
        pos = ends[which]
        lists[pos] = ((what >> 9) << 9) | (q << 6) | (p << 3) | n
        coefs[pos] = fk[p, n]
        one = nl[p, n] & lv[p] & what & 1
        ends[which] = pos + one
        s = what >> 9
        late = s >= EARLY
        which = jnp.where((what & 2) != 0, jnp.where(late, 5, 4), 6)
        pos = ends[which]
        lists[pos] = (jnp.where(late, s - EARLY, s) << 9) | (q << 6) | (p << 3) | n
        coefs[pos] = fk[p, n]
        ends[which] = pos + one
        return 0

    lax.fori_loop(0, 64, entry, 0, unroll=4)
    for k in range(LISTS - 1):
        e = ends[k]
        lists[COUNTS + k] = e - k * CAP
        for u in range(LONG):
            lists[e + u] = base << 3
            coefs[e + u] = 0.0
    for p in range(8):
        lists[LIVE + p] = lv[p]
        coefs[GAP + p] = gp[p]
    for c in tiles[4:] + slabs:
        c.wait()


def step(at, size, lists, coefs, inter, src, acc):
    for u in range(size):
        code = lists[at + u]
        n, p, q, s = code & 7, (code >> 3) & 7, (code >> 6) & 7, code >> 9
        x = inter[p, n]
        h = jnp.dot(x, src[s], preferred_element_type=F32).astype(BF16)
        t = lax.dot_general(h, x, (((1,), (1,)), ((), ())), preferred_element_type=F32)
        acc[q] = acc[q] - coefs[at + u] * t


def steps(at, count, size, *refs):
    def body(i, _):
        step(at + i * size, size, *refs)
        return 0

    lax.fori_loop(0, count, body, 0)


def long_list(which, lists, *refs):
    at, count = which * CAP, lists[COUNTS + which]
    longs = (count + LONG - SHORT - 1) // LONG
    steps(at, longs, LONG, lists, *refs)
    left = jnp.maximum(count - longs * LONG + SHORT - 1, 0)
    steps(at + longs * LONG, left // SHORT, SHORT, lists, *refs)


def across_list_tail(which, lists, *refs):
    more = jnp.maximum(lists[COUNTS + which] - 1, 0) // SHORT
    steps(which * CAP + SHORT, more, SHORT, lists, *refs)


def gather(src, xs, ia, ib, iha, ihb):
    at = 0
    for x in xs:
        src[at : at + x.shape[0]] = x[...]
        at += x.shape[0]
    src[4:6] = ia[...]
    src[6:8] = ib[...]
    src[8:10] = iha[...]
    src[10:12] = ihb[...]


def start_half(half, lists, coefs, exch, energy, acc, amps, recip):
    slots = slots_of(4 * half, 4 * half + 4)
    dens = denominators(energy, [coefs[GAP + p] for p in slots], slots)
    for j, p in enumerate(slots):
        q = 4 * half + j
        ex = exch[p].astype(F32)
        a0 = -lists[LIVE + p].astype(F32) * ex / dens[j]
        amps[q] = a0
        recip[q] = 1.0 / dens[j]
        acc[q] = ex + dens[j] * a0


def update_half(half, lists, acc, amps, recip, out):
    places = [o.at[k] for o in out for k in range(o.shape[0])]
    for j, p in enumerate(slots_of(4 * half, 4 * half + 4)):
        q = 4 * half + j
        res = lists[LIVE + p].astype(F32) * acc[q]
        a1 = amps[q] - res * recip[q]
        amps[q] = a1
        places[j][...] = a1.astype(BF16)


def waits_longer():
    return ((lax.axis_index("row") + 1) & 2) != 0


def near_kernel_1(lists, coefs, inter_hbm, exch, energy, x, ia, ib, iha, ihb, inter_in, acc, amps, recip, src, inter, sem):
    del inter_in
    slabs = start_all([(inter_hbm.at[p], inter.at[p]) for p in slots_of(4, 8)], sem)
    gather(src, [x], ia, ib, iha, ihb)
    start_half(0, lists, coefs, exch, energy, acc, amps, recip)
    long_list(0, lists, coefs, inter, src, acc)
    for c in slabs:
        c.wait()

    @pl.when(waits_longer())
    def _():
        start_half(1, lists, coefs, exch, energy, acc, amps, recip)
        long_list(1, lists, coefs, inter, src, acc)


def across_kernel(lists, coefs, inter, xh, recip, acc_in, amps_in, out_a, out_b, acc, amps):
    del acc_in, amps_in
    refs = (lists, coefs, inter, xh, acc)
    across_list_tail(2, *refs)
    step(2 * CAP, SHORT, *refs)
    update_half(0, lists, acc, amps, recip, [out_a, out_b])


def rest_kernel(lists, coefs, inter, exch, energy, src, xh, acc_in, amps_in, recip_in, out_a, out_b, acc, amps, recip):
    del acc_in, amps_in, recip_in

    @pl.when(jnp.logical_not(waits_longer()))
    def _():
        start_half(1, lists, coefs, exch, energy, acc, amps, recip)
        long_list(1, lists, coefs, inter, src, acc)

    refs = (lists, coefs, inter, xh, acc)
    across_list_tail(3, *refs)
    step(3 * CAP, SHORT, *refs)
    update_half(1, lists, acc, amps, recip, [out_a, out_b])


def squares(res):
    s = jnp.sum((res * res).reshape(32, 8, 256), axis=0)
    return s[:, :128] + s[:, 128:]


def near_kernel_2(lists, coefs, inter, exch, energy, xa, xb, ia, ib, iha, ihb, amps, acc_in, acc, sq, src):
    del acc_in
    slots = slots_of(0, 8)
    dens = denominators(energy, [coefs[GAP + p] for p in slots], slots)
    total = jnp.zeros((8, 128), F32)
    for q, p in enumerate(slots):
        total = total + squares(lists[LIVE + p].astype(F32) * acc[q])
        acc[q] = exch[p].astype(F32) + dens[q] * amps[q]
    sq[...] = total
    gather(src, [xa, xb], ia, ib, iha, ihb)
    for half in range(2):
        long_list(half, lists, coefs, inter, src, acc)


def early_kernel(lists, coefs, inter, xh, acc_in, acc):
    del acc_in
    long_list(4, lists, coefs, inter, xh, acc)


def last_kernel(lists, coefs, inter, xh, recip, amps, sq1, acc_in, out, sums, acc, buf, sem):
    del acc_in
    total = jnp.zeros((8, 128), F32)
    copies = []
    refs = (lists, coefs, inter, xh, acc)
    across_list_tail(5, *refs)
    step(5 * CAP, SHORT, *refs)
    for q, p in enumerate(slots_of(0, 8)):
        res = lists[LIVE + p].astype(F32) * acc[q]
        total = total + squares(res)
        buf[q] = amps[q] - res * recip[q]
        copies.append(pltpu.make_async_copy(buf.at[q], out.at[p], sem.at[q]))
        copies[-1].start()
    rows = (sums.shape[0], 128)
    sums[:, :128] = jnp.broadcast_to(jnp.sum(sq1[...], axis=0, keepdims=True), rows)
    sums[:, 128:] = jnp.broadcast_to(jnp.sum(total, axis=0, keepdims=True), rows)
    for c in copies:
        c.wait()


def on_device(amp_exch, pno_energy, pair_gap, fock, intersection, nbr_slot, nbr_live, pair_live):
    count = lax.axis_size("row")
    v = amp_exch.shape[-1]
    tiles4 = pltpu.VMEM((4, v, v), BF16)
    tiles8 = pltpu.VMEM((8, v, v), F32)
    dma = pltpu.SemaphoreType.DMA
    per_pair = [pltpu.SMEM((8,), F32), pltpu.SMEM((8,), jnp.int32)]
    same_chip = [(i, i ^ 1) for i in range(count) if (i ^ 1) < count]
    other_chip = [(i, i + 1) for i in range(1, count - 1, 2)]
    other_chip += [(j, i) for i, j in other_chip]
    big = [hbm(a) for a in (amp_exch, pno_energy, pair_gap, pair_live, fock, nbr_slot, nbr_live)]

    tiles2 = pltpu.VMEM((2, v, v), BF16)
    slabs = pltpu.VMEM(intersection.shape, BF16)
    intersection = hbm(intersection)
    x0 = pl.pallas_call(
        first_kernel, out_shape=tiles4, in_specs=[AN] * 4, out_specs=VM,
        scratch_shapes=[pltpu.VMEM((4, v, v), BF16), pltpu.VMEM((8, v), F32)] + per_pair + [dma((4,)), dma((3,))],
        compiler_params=params(8), cost_estimate=COST, name="first",
    )(*big[:4])
    xh = lax.ppermute(x0, "row", other_chip)
    i0a, i0b, exch, energy, lists, coefs, inter = pl.pallas_call(
        second_kernel,
        out_shape=[tiles2, tiles2, pltpu.VMEM((8, v, v), BF16), pltpu.VMEM((8, v), F32),
                   pltpu.SMEM((LIVE + 8,), jnp.int32), pltpu.SMEM((GAP + 8,), F32), slabs],
        in_specs=[AN] * 9, out_specs=[VM] * 4 + [SM] * 2 + [VM],
        scratch_shapes=per_pair + [pltpu.SMEM((8, 8), F32)] + [pltpu.SMEM((8, 8), jnp.int32)] * 2
        + [pltpu.SMEM((24,), jnp.int32), pltpu.SMEM((LISTS,), jnp.int32), dma((8,)), dma((6,)), dma((4,))],
        compiler_params=params(8), cost_estimate=COST, name="second",
    )(*big, intersection, x0)

    def swap(*halves):
        return [vmem(lax.ppermute(h, "row", same_chip)) for h in halves]

    meta = (lists, coefs)
    exch, energy = vmem(exch), vmem(energy)
    gathered = pltpu.VMEM((12, v, v), BF16)
    acc, amps, recip, src, inter = pl.pallas_call(
        near_kernel_1, out_shape=[tiles8] * 3 + [gathered, slabs], in_specs=[SM] * 2 + [AN] + [VM] * 8, out_specs=[VM] * 5,
        scratch_shapes=[dma((4,))], input_output_aliases={10: 4},
        compiler_params=params(8), cost_estimate=COST, name="near1",
    )(*meta, intersection, exch, energy, vmem(x0), vmem(i0a), vmem(i0b), *swap(i0a, i0b), vmem(inter))
    inter = vmem(inter)
    early, late = pltpu.VMEM((EARLY, v, v), BF16), pltpu.VMEM((4 - EARLY, v, v), BF16)
    x1a, x1b, acc, amps = pl.pallas_call(
        across_kernel, out_shape=[early, late, tiles8, tiles8],
        in_specs=[SM] * 2 + [VM] * 5, out_specs=[VM] * 4, input_output_aliases={5: 2, 6: 3},
        compiler_params=params(8), cost_estimate=COST, name="across",
    )(*meta, inter, vmem(xh), vmem(recip), vmem(acc), vmem(amps))
    xh1a = lax.ppermute(x1a, "row", other_chip)
    xh1b = lax.ppermute(x1b, "row", other_chip)
    i1a, i1b, acc, amps, recip = pl.pallas_call(
        rest_kernel, out_shape=[tiles2, tiles2] + [tiles8] * 3,
        in_specs=[SM] * 2 + [VM] * 8, out_specs=[VM] * 5, input_output_aliases={7: 2, 8: 3, 9: 4},
        compiler_params=params(8), cost_estimate=COST, name="rest",
    )(*meta, inter, exch, energy, vmem(src), vmem(xh), vmem(acc), vmem(amps), vmem(recip))
    acc, sq = pl.pallas_call(
        near_kernel_2, out_shape=[tiles8, pltpu.VMEM((8, 128), F32)], in_specs=[SM] * 2 + [VM] * 11, out_specs=[VM] * 2,
        scratch_shapes=[gathered], input_output_aliases={12: 0},
        compiler_params=params(8), cost_estimate=COST, name="near2",
    )(*meta, inter, exch, energy, vmem(x1a), vmem(x1b), vmem(i1a), vmem(i1b), *swap(i1a, i1b), vmem(amps), vmem(acc))
    acc = pl.pallas_call(
        early_kernel, out_shape=tiles8, in_specs=[SM] * 2 + [VM] * 3, out_specs=VM, input_output_aliases={4: 0},
        compiler_params=params(8), cost_estimate=COST, name="early",
    )(*meta, inter, vmem(xh1a), vmem(acc))
    out, sums, _ = pl.pallas_call(
        last_kernel, out_shape=[jax.ShapeDtypeStruct((8, v, v), F32), pltpu.VMEM((count, 256), F32), tiles8],
        in_specs=[SM] * 2 + [VM] * 6, out_specs=[AN, VM, VM], input_output_aliases={7: 2},
        scratch_shapes=[pltpu.VMEM((8, v, v), F32), dma((8,))],
        compiler_params=params(8), cost_estimate=COST, name="last",
    )(*meta, inter, vmem(xh1b), vmem(recip), vmem(amps), vmem(sq), vmem(acc))
    sums = lax.all_to_all(sums, "row", 0, 0, tiled=True)
    norms = jnp.sqrt(jnp.sum(sums.reshape(count, 2, 128), axis=(0, 2)) / (amp_exch.shape[0] * count * v * v))
    return out, norms


def solution(mesh):
    whole = P(("grp", "row"))
    return jax.shard_map(
        on_device, mesh=mesh, in_specs=(whole,) * 8, out_specs=(whole, P("grp")), check_vma=False
    )
```

```python
import functools

import jax
import jax.numpy as jnp
from jax import lax
from jax.experimental import pallas as pl
from jax.experimental.pallas import tpu as pltpu
from jax.sharding import PartitionSpec as P

F32 = jnp.float32
BF16 = jnp.bfloat16
VM = pl.BlockSpec(memory_space=pltpu.VMEM)
SM = pl.BlockSpec(memory_space=pltpu.SMEM)
AN = pl.BlockSpec(memory_space=pl.ANY)
CAP = 80
LONG, SHORT, FEW = 16, 8, 4
LOCAL, NEAR, ACROSS, FIRST_PART, SECOND_PART, LISTS = 0, 2, 4, 6, 7, 10
COUNTS, LIVE = LISTS * CAP, LISTS * CAP + LISTS
GAP = LISTS * CAP
EARLY = 3
MIB = 1 << 20


def base_slot():
    return lax.rem(lax.axis_index("row"), 2) * 4


def slots_of(first, end):
    base = base_slot()
    return [(q + base) & 7 for q in range(first, end)]


def params(mib, **kw):
    return pltpu.CompilerParams(vmem_limit_bytes=mib * MIB, **kw)


COST = pl.CostEstimate(flops=1000, bytes_accessed=1000, transcendentals=0)


def vmem(x):
    return pltpu.with_memory_space_constraint(x, pltpu.VMEM)


def hbm(x):
    return pltpu.with_memory_space_constraint(x, pltpu.HBM)


def denominators(energy, gaps, slots):
    rows = [energy[pl.ds(p, 1), :] for p in slots]
    fill = [jnp.zeros_like(rows[0])] * (8 - len(rows))
    cols = jnp.transpose(jnp.concatenate(rows + fill, axis=0))
    return [cols[:, i : i + 1] + rows[i] + gaps[i] for i in range(len(slots))]


def start_all(pairs, sems):
    copies = [pltpu.make_async_copy(a, b, sems.at[i]) for i, (a, b) in enumerate(pairs)]
    for c in copies:
        c.start()
    return copies


def first_kernel(exch, energy, gap, live, out, buf, en, gp, lv, sem, sems):
    slots = slots_of(0, 4)
    small = start_all([(energy, en), (gap, gp), (live, lv)], sems)
    tiles = start_all([(exch.at[p], buf.at[i]) for i, p in enumerate(slots)], sem)
    for c in small:
        c.wait()
    dens = denominators(en, [gp[p] for p in slots], slots)
    for i, p in enumerate(slots):
        tiles[i].wait()
        out[i] = (-lv[p].astype(F32) * buf[i].astype(F32) / dens[i]).astype(BF16)


def second_kernel(
    exch, energy, gap, live, fock, nslot, nlive, inter_hbm, x, out_a, out_b, ex, en, lists, coefs, inter,
    gp, lv, fk, ns, nl, table, ends, sem, sems, slab_sem,
):
    del x
    slots = slots_of(4, 8)
    base = base_slot()
    small = start_all([(energy, en), (gap, gp), (live, lv), (fock, fk), (nslot, ns), (nlive, nl)], sems)
    order = slots + slots_of(0, 4)
    tiles = start_all([(exch.at[p], ex.at[p]) for p in order], sem)
    slabs = start_all([(inter_hbm.at[p], inter.at[p]) for p in order[4:]], slab_sem)
    for c in small:
        c.wait()
    dens = denominators(en, [gp[p] for p in slots], slots)
    for i, p in enumerate(slots):
        tiles[i].wait()
        tile = (-lv[p].astype(F32) * ex[p].astype(F32) / dens[i]).astype(BF16)
        if i < 2:
            out_a[i] = tile
        else:
            out_b[i - 2] = tile

    for s in range(4):
        table[4 + s] = (s << 9) | 1 | jnp.where(base == 0, ACROSS, NEAR) << 1
        table[16 + s] = (s << 9) | 1 | jnp.where(base == 0, NEAR, ACROSS) << 1
    for s in range(8):
        table[8 + s] = (((s + base) & 7) << 9) | lv[s]
    for k in range(LISTS):
        ends[k] = k * CAP

    def entry(i, _):
        q, n = i >> 3, i & 7
        p = (q + base) & 7
        what = table[ns[p, n]]
        kind, half, s = (what >> 1) & 7, q >> 2, what >> 9
        late = s >= EARLY
        again = jnp.where(kind == ACROSS, jnp.where(late, SECOND_PART + half, FIRST_PART), LISTS - 1)
        low = (q << 6) | (p << 3) | n
        one = nl[p, n] & lv[p] & what & 1
        for which, place in ((kind + half, s), (again, jnp.where(late, s - EARLY, s))):
            pos = ends[which]
            lists[pos] = (place << 9) | low
            coefs[pos] = fk[p, n]
            ends[which] = pos + one
        return 0

    lax.fori_loop(0, 64, entry, 0, unroll=4)
    for k in range(LISTS - 1):
        e = ends[k]
        lists[COUNTS + k] = e - k * CAP
        for u in range(LONG):
            lists[e + u] = base << 3
            coefs[e + u] = 0.0
    for p in range(8):
        lists[LIVE + p] = lv[p]
        coefs[GAP + p] = gp[p]
    for c in tiles[4:] + slabs:
        c.wait()


def step(at, size, lists, coefs, inter, src, acc):
    for u in range(size):
        code = lists[at + u]
        n, p, q, s = code & 7, (code >> 3) & 7, (code >> 6) & 7, code >> 9
        x = inter[p, n]
        h = jnp.dot(x, src[s], preferred_element_type=F32).astype(BF16)
        t = lax.dot_general(h, x, (((1,), (1,)), ((), ())), preferred_element_type=F32)
        acc[q] = acc[q] - coefs[at + u] * t


def steps(at, count, size, *refs):
    def body(i, _):
        step(at + i * size, size, *refs)
        return 0

    lax.fori_loop(0, count, body, 0)


def long_list(which, lists, *refs):
    at, count = which * CAP, lists[COUNTS + which]
    longs = (count + LONG - SHORT - 1) // LONG
    steps(at, longs, LONG, lists, *refs)
    left = jnp.maximum(count - longs * LONG + SHORT - 1, 0)
    steps(at + longs * LONG, left // SHORT, SHORT, lists, *refs)


def list_tail(which, size, lists, *refs):
    more = jnp.maximum(lists[COUNTS + which] - 1, 0) // size
    steps(which * CAP + size, more, size, lists, *refs)


def gather(src, *parts):
    at = 0
    for x in parts:
        src[at : at + x.shape[0]] = x[...]
        at += x.shape[0]


def start_half(half, lists, coefs, exch, energy, acc, amps, recip):
    slots = slots_of(4 * half, 4 * half + 4)
    dens = denominators(energy, [coefs[GAP + p] for p in slots], slots)
    for j, p in enumerate(slots):
        q = 4 * half + j
        ex = exch[p].astype(F32)
        a0 = -lists[LIVE + p].astype(F32) * ex / dens[j]
        amps[q] = a0
        recip[q] = 1.0 / dens[j]
        acc[q] = ex + dens[j] * a0


def update_half(half, lists, acc, amps, recip, out):
    places = [o.at[k] for o in out for k in range(o.shape[0])]
    for j, p in enumerate(slots_of(4 * half, 4 * half + 4)):
        q = 4 * half + j
        res = lists[LIVE + p].astype(F32) * acc[q]
        a1 = amps[q] - res * recip[q]
        amps[q] = a1
        places[j][...] = a1.astype(BF16)


def waits_longer():
    return ((lax.axis_index("row") + 1) & 2) != 0


def local_kernel_1(lists, coefs, inter_hbm, exch, energy, x, ia, ib, inter_in, acc, amps, recip, src, inter, sem):
    del inter_in
    slabs = start_all([(inter_hbm.at[p], inter.at[p]) for p in slots_of(4, 8)], sem)
    gather(src, x, ia, ib)
    start_half(0, lists, coefs, exch, energy, acc, amps, recip)
    long_list(LOCAL, lists, coefs, inter, src, acc)
    for c in slabs:
        c.wait()

    @pl.when(waits_longer())
    def _():
        start_half(1, lists, coefs, exch, energy, acc, amps, recip)
        long_list(LOCAL + 1, lists, coefs, inter, src, acc)


def near_kernel_1(lists, coefs, inter, iha, ihb, acc_in, acc, ih):
    del acc_in
    gather(ih, iha, ihb)
    long_list(NEAR, lists, coefs, inter, ih, acc)

    @pl.when(waits_longer())
    def _():
        long_list(NEAR + 1, lists, coefs, inter, ih, acc)


def across_kernel(lists, coefs, inter, xh, recip, acc_in, amps_in, out_a, out_b, acc, amps):
    del acc_in, amps_in
    refs = (lists, coefs, inter, xh, acc)
    list_tail(ACROSS, SHORT, *refs)
    step(ACROSS * CAP, SHORT, *refs)
    update_half(0, lists, acc, amps, recip, [out_a, out_b])


def rest_kernel(lists, coefs, inter, exch, energy, src, ih, xh, acc_in, amps_in, recip_in, out_a, out_b, acc, amps, recip):
    del acc_in, amps_in, recip_in

    @pl.when(jnp.logical_not(waits_longer()))
    def _():
        start_half(1, lists, coefs, exch, energy, acc, amps, recip)
        long_list(LOCAL + 1, lists, coefs, inter, src, acc)
        long_list(NEAR + 1, lists, coefs, inter, ih, acc)

    refs = (lists, coefs, inter, xh, acc)
    list_tail(ACROSS + 1, SHORT, *refs)
    step((ACROSS + 1) * CAP, SHORT, *refs)
    update_half(1, lists, acc, amps, recip, [out_a, out_b])


def squares(res):
    s = jnp.sum((res * res).reshape(32, 8, 256), axis=0)
    return s[:, :128] + s[:, 128:]


def local_kernel_2(lists, coefs, inter, exch, energy, xa, xb, ia, ib, amps, acc_in, acc, sq, src):
    del acc_in
    slots = slots_of(0, 8)
    dens = denominators(energy, [coefs[GAP + p] for p in slots], slots)
    total = jnp.zeros((8, 128), F32)
    for q, p in enumerate(slots):
        total = total + squares(lists[LIVE + p].astype(F32) * acc[q])
        acc[q] = exch[p].astype(F32) + dens[q] * amps[q]
    sq[...] = total
    gather(src, xa, xb, ia, ib)
    for half in range(2):
        long_list(LOCAL + half, lists, coefs, inter, src, acc)


def near_kernel_2(lists, coefs, inter, iha, ihb, acc_in, acc, ih):
    del acc_in
    gather(ih, iha, ihb)
    for half in range(2):
        long_list(NEAR + half, lists, coefs, inter, ih, acc)


def early_kernel(lists, coefs, inter, xh, acc_in, acc):
    del acc_in
    long_list(FIRST_PART, lists, coefs, inter, xh, acc)


def last_kernel(lists, coefs, inter, xh, recip, amps, sq1, acc_in, out, sums, acc, buf, sem):
    del acc_in
    total = jnp.zeros((8, 128), F32)
    copies = []
    refs = (lists, coefs, inter, xh, acc)
    slots = slots_of(0, 8)
    for half in range(2):
        list_tail(SECOND_PART + half, FEW, *refs)
    for half in range(2):
        step((SECOND_PART + half) * CAP, FEW, *refs)
        for q in range(4 * half, 4 * half + 4):
            p = slots[q]
            res = lists[LIVE + p].astype(F32) * acc[q]
            total = total + squares(res)
            buf[q] = amps[q] - res * recip[q]
            copies.append(pltpu.make_async_copy(buf.at[q], out.at[p], sem.at[q]))
            copies[-1].start()
    rows = (sums.shape[0], 128)
    sums[:, :128] = jnp.broadcast_to(jnp.sum(sq1[...], axis=0, keepdims=True), rows)
    sums[:, 128:] = jnp.broadcast_to(jnp.sum(total, axis=0, keepdims=True), rows)
    for c in copies:
        c.wait()


def on_device(amp_exch, pno_energy, pair_gap, fock, intersection, nbr_slot, nbr_live, pair_live):
    count = lax.axis_size("row")
    v = amp_exch.shape[-1]
    tiles4 = pltpu.VMEM((4, v, v), BF16)
    tiles8 = pltpu.VMEM((8, v, v), F32)
    dma = pltpu.SemaphoreType.DMA
    per_pair = [pltpu.SMEM((8,), F32), pltpu.SMEM((8,), jnp.int32)]
    same_chip = [(i, i ^ 1) for i in range(count) if (i ^ 1) < count]
    other_chip = [(i, i + 1) for i in range(1, count - 1, 2)]
    other_chip += [(j, i) for i, j in other_chip]
    big = [hbm(a) for a in (amp_exch, pno_energy, pair_gap, pair_live, fock, nbr_slot, nbr_live)]

    tiles2 = pltpu.VMEM((2, v, v), BF16)
    slabs = pltpu.VMEM(intersection.shape, BF16)
    intersection = hbm(intersection)
    x0 = pl.pallas_call(
        first_kernel, out_shape=tiles4, in_specs=[AN] * 4, out_specs=VM,
        scratch_shapes=[pltpu.VMEM((4, v, v), BF16), pltpu.VMEM((8, v), F32)] + per_pair + [dma((4,)), dma((3,))],
        compiler_params=params(8), cost_estimate=COST, name="first",
    )(*big[:4])
    xh = lax.ppermute(x0, "row", other_chip)
    i0a, i0b, exch, energy, lists, coefs, inter = pl.pallas_call(
        second_kernel,
        out_shape=[tiles2, tiles2, pltpu.VMEM((8, v, v), BF16), pltpu.VMEM((8, v), F32),
                   pltpu.SMEM((LIVE + 8,), jnp.int32), pltpu.SMEM((GAP + 8,), F32), slabs],
        in_specs=[AN] * 9, out_specs=[VM] * 4 + [SM] * 2 + [VM],
        scratch_shapes=per_pair + [pltpu.SMEM((8, 8), F32)] + [pltpu.SMEM((8, 8), jnp.int32)] * 2
        + [pltpu.SMEM((24,), jnp.int32), pltpu.SMEM((LISTS,), jnp.int32), dma((8,)), dma((6,)), dma((4,))],
        compiler_params=params(8), cost_estimate=COST, name="second",
    )(*big, intersection, x0)

    def swap(*halves):
        return [vmem(lax.ppermute(h, "row", same_chip)) for h in halves]

    meta = (lists, coefs)
    exch, energy = vmem(exch), vmem(energy)
    own = pltpu.VMEM((8, v, v), BF16)
    acc, amps, recip, src, inter = pl.pallas_call(
        local_kernel_1, out_shape=[tiles8] * 3 + [own, slabs], in_specs=[SM] * 2 + [AN] + [VM] * 6, out_specs=[VM] * 5,
        scratch_shapes=[dma((4,))], input_output_aliases={8: 4},
        compiler_params=params(8), cost_estimate=COST, name="local1",
    )(*meta, intersection, exch, energy, vmem(x0), vmem(i0a), vmem(i0b), vmem(inter))
    inter = vmem(inter)
    acc, ih = pl.pallas_call(
        near_kernel_1, out_shape=[tiles8, tiles4], in_specs=[SM] * 2 + [VM] * 4, out_specs=[VM] * 2, input_output_aliases={5: 0},
        compiler_params=params(8), cost_estimate=COST, name="near1",
    )(*meta, inter, *swap(i0a, i0b), vmem(acc))
    early, late = pltpu.VMEM((EARLY, v, v), BF16), pltpu.VMEM((4 - EARLY, v, v), BF16)
    x1a, x1b, acc, amps = pl.pallas_call(
        across_kernel, out_shape=[early, late, tiles8, tiles8],
        in_specs=[SM] * 2 + [VM] * 5, out_specs=[VM] * 4, input_output_aliases={5: 2, 6: 3},
        compiler_params=params(8), cost_estimate=COST, name="across",
    )(*meta, inter, vmem(xh), vmem(recip), vmem(acc), vmem(amps))
    xh1a = lax.ppermute(x1a, "row", other_chip)
    xh1b = lax.ppermute(x1b, "row", other_chip)
    i1a, i1b, acc, amps, recip = pl.pallas_call(
        rest_kernel, out_shape=[tiles2, tiles2] + [tiles8] * 3,
        in_specs=[SM] * 2 + [VM] * 9, out_specs=[VM] * 5, input_output_aliases={8: 2, 9: 3, 10: 4},
        compiler_params=params(8), cost_estimate=COST, name="rest",
    )(*meta, inter, exch, energy, vmem(src), vmem(ih), vmem(xh), vmem(acc), vmem(amps), vmem(recip))
    acc, sq = pl.pallas_call(
        local_kernel_2, out_shape=[tiles8, pltpu.VMEM((8, 128), F32)], in_specs=[SM] * 2 + [VM] * 9, out_specs=[VM] * 2,
        scratch_shapes=[own], input_output_aliases={10: 0},
        compiler_params=params(8), cost_estimate=COST, name="local2",
    )(*meta, inter, exch, energy, vmem(x1a), vmem(x1b), vmem(i1a), vmem(i1b), vmem(amps), vmem(acc))
    acc = pl.pallas_call(
        near_kernel_2, out_shape=tiles8, in_specs=[SM] * 2 + [VM] * 4, out_specs=VM, input_output_aliases={5: 0},
        scratch_shapes=[tiles4], compiler_params=params(8), cost_estimate=COST, name="near2",
    )(*meta, inter, *swap(i1a, i1b), vmem(acc))
    acc = pl.pallas_call(
        early_kernel, out_shape=tiles8, in_specs=[SM] * 2 + [VM] * 3, out_specs=VM, input_output_aliases={4: 0},
        compiler_params=params(8), cost_estimate=COST, name="early",
    )(*meta, inter, vmem(xh1a), vmem(acc))
    out, sums, _ = pl.pallas_call(
        last_kernel, out_shape=[jax.ShapeDtypeStruct((8, v, v), F32), pltpu.VMEM((count, 256), F32), tiles8],
        in_specs=[SM] * 2 + [VM] * 6, out_specs=[AN, VM, VM], input_output_aliases={7: 2},
        scratch_shapes=[pltpu.VMEM((8, v, v), F32), dma((8,))],
        compiler_params=params(8), cost_estimate=COST, name="last",
    )(*meta, inter, vmem(xh1b), vmem(recip), vmem(amps), vmem(sq), vmem(acc))
    sums = lax.all_to_all(sums, "row", 0, 0, tiled=True)
    norms = jnp.sqrt(jnp.sum(sums.reshape(count, 2, 128), axis=(0, 2)) / (amp_exch.shape[0] * count * v * v))
    return out, norms


def solution(mesh):
    whole = P(("grp", "row"))
    return jax.shard_map(
        on_device, mesh=mesh, in_specs=(whole,) * 8, out_specs=(whole, P("grp")), check_vma=False
    )
```

```python
import functools

import jax
import jax.numpy as jnp
from jax import lax
from jax.experimental import pallas as pl
from jax.experimental.pallas import tpu as pltpu
from jax.sharding import PartitionSpec as P

F32 = jnp.float32
BF16 = jnp.bfloat16
VM = pl.BlockSpec(memory_space=pltpu.VMEM)
SM = pl.BlockSpec(memory_space=pltpu.SMEM)
AN = pl.BlockSpec(memory_space=pl.ANY)
CAP = 72
LONG, SHORT = 16, 8
COUNTS, LIVE = 4 * CAP, 4 * CAP + 4
GAP = 4 * CAP
MIB = 1 << 20


def base_slot():
    return lax.rem(lax.axis_index("row"), 2) * 4


def slots_of(first, end):
    base = base_slot()
    return [(q + base) & 7 for q in range(first, end)]


def params(mib, **kw):
    return pltpu.CompilerParams(vmem_limit_bytes=mib * MIB, **kw)


COST = pl.CostEstimate(flops=1000, bytes_accessed=1000, transcendentals=0)


def vmem(x):
    return pltpu.with_memory_space_constraint(x, pltpu.VMEM)


def hbm(x):
    return pltpu.with_memory_space_constraint(x, pltpu.HBM)


def denominators(energy, gaps, slots):
    rows = [energy[pl.ds(p, 1), :] for p in slots]
    fill = [jnp.zeros_like(rows[0])] * (8 - len(rows))
    cols = jnp.transpose(jnp.concatenate(rows + fill, axis=0))
    return [cols[:, i : i + 1] + rows[i] + gaps[i] for i in range(len(slots))]


def start_all(pairs, sems):
    copies = [pltpu.make_async_copy(a, b, sems.at[i]) for i, (a, b) in enumerate(pairs)]
    for c in copies:
        c.start()
    return copies


def first_kernel(exch, energy, gap, live, out, buf, en, gp, lv, sem, sems):
    slots = slots_of(0, 4)
    small = start_all([(energy, en), (gap, gp), (live, lv)], sems)
    tiles = start_all([(exch.at[p], buf.at[i]) for i, p in enumerate(slots)], sem)
    for c in small:
        c.wait()
    dens = denominators(en, [gp[p] for p in slots], slots)
    factors = [-lv[p].astype(F32) / dens[i] for i, p in enumerate(slots)]
    for i in range(4):
        tiles[i].wait()
        out[i] = (buf[i].astype(F32) * factors[i]).astype(BF16)


def second_kernel(
    exch, energy, gap, live, fock, nslot, nlive, inter_hbm, x, out_a, out_b, ex, en, lists, coefs, inter,
    gp, lv, fk, ns, nl, table, ends, sem, sems, slab_sem,
):
    del x
    slots = slots_of(4, 8)
    base = base_slot()
    small = start_all([(energy, en), (gap, gp), (live, lv), (fock, fk), (nslot, ns), (nlive, nl)], sems)
    order = slots + slots_of(0, 4)
    tiles = start_all([(exch.at[p], ex.at[p]) for p in order], sem)
    slabs = start_all([(inter_hbm.at[p], inter.at[p]) for p in order[4:]], slab_sem)
    for c in small:
        c.wait()
    dens = denominators(en, [gp[p] for p in slots], slots)
    for i, p in enumerate(slots):
        tiles[i].wait()
        tile = (-lv[p].astype(F32) * ex[p].astype(F32) / dens[i]).astype(BF16)
        if i < 2:
            out_a[i] = tile
        else:
            out_b[i - 2] = tile

    for s in range(4):
        table[4 + s] = jnp.where(base == 0, (s << 9) | 3, ((8 + s) << 9) | 1)
        table[16 + s] = jnp.where(base == 0, ((8 + s) << 9) | 1, (s << 9) | 3)
    for s in range(8):
        table[8 + s] = (((s + base) & 7) << 9) | lv[s]
    for k in range(4):
        ends[k] = k * CAP

    def entry(i, _):
        q, n = i >> 3, i & 7
        p = (q + base) & 7
        what = table[ns[p, n]]
        which = (what & 2) + (q >> 2)
        pos = ends[which]
        lists[pos] = ((what >> 9) << 9) | (q << 6) | (p << 3) | n
        coefs[pos] = fk[p, n]
        ends[which] = pos + (nl[p, n] & lv[p] & what & 1)
        return 0

    lax.fori_loop(0, 64, entry, 0, unroll=4)
    for k in range(4):
        e = ends[k]
        lists[COUNTS + k] = e - k * CAP
        for u in range(LONG):
            lists[e + u] = base << 3
            coefs[e + u] = 0.0
    for p in range(8):
        lists[LIVE + p] = lv[p]
        coefs[GAP + p] = gp[p]
    for c in tiles[4:] + slabs:
        c.wait()


def step(at, size, lists, coefs, inter, src, acc):
    for u in range(size):
        code = lists[at + u]
        n, p, q, s = code & 7, (code >> 3) & 7, (code >> 6) & 7, code >> 9
        x = inter[p, n]
        h = jnp.dot(x, src[s], preferred_element_type=F32).astype(BF16)
        t = lax.dot_general(h, x, (((1,), (1,)), ((), ())), preferred_element_type=F32)
        acc[q] = acc[q] - coefs[at + u] * t


def steps(at, count, size, *refs):
    def body(i, _):
        step(at + i * size, size, *refs)
        return 0

    lax.fori_loop(0, count, body, 0)


def near_list(which, lists, *refs):
    at, count = which * CAP, lists[COUNTS + which]
    longs = (count + LONG - SHORT - 1) // LONG
    steps(at, longs, LONG, lists, *refs)
    left = jnp.maximum(count - longs * LONG + SHORT - 1, 0)
    steps(at + longs * LONG, left // SHORT, SHORT, lists, *refs)


def across_list_tail(which, lists, *refs):
    more = jnp.maximum(lists[COUNTS + which] - 1, 0) // SHORT
    steps(which * CAP + SHORT, more, SHORT, lists, *refs)


def gather(src, x, ia, ib, iha, ihb):
    src[0:4] = x[...]
    src[4:6] = ia[...]
    src[6:8] = ib[...]
    src[8:10] = iha[...]
    src[10:12] = ihb[...]


def start_half(half, lists, coefs, exch, energy, acc, amps, recip):
    slots = slots_of(4 * half, 4 * half + 4)
    dens = denominators(energy, [coefs[GAP + p] for p in slots], slots)
    for j, p in enumerate(slots):
        q = 4 * half + j
        ex = exch[p].astype(F32)
        a0 = -lists[LIVE + p].astype(F32) * ex / dens[j]
        amps[q] = a0
        recip[q] = 1.0 / dens[j]
        acc[q] = ex + dens[j] * a0


def update_half(half, lists, acc, amps, recip, out):
    each = 4 // len(out)
    for j, p in enumerate(slots_of(4 * half, 4 * half + 4)):
        q = 4 * half + j
        res = lists[LIVE + p].astype(F32) * acc[q]
        a1 = amps[q] - res * recip[q]
        amps[q] = a1
        out[j // each][j % each] = a1.astype(BF16)


def waits_longer():
    return ((lax.axis_index("row") + 1) & 2) != 0


def near_kernel_1(lists, coefs, inter_hbm, exch, energy, x, ia, ib, iha, ihb, inter_in, acc, amps, recip, src, inter, sem):
    del inter_in
    slabs = start_all([(inter_hbm.at[p], inter.at[p]) for p in slots_of(4, 8)], sem)
    gather(src, x, ia, ib, iha, ihb)
    start_half(0, lists, coefs, exch, energy, acc, amps, recip)
    near_list(0, lists, coefs, inter, src, acc)
    for c in slabs:
        c.wait()

    @pl.when(waits_longer())
    def _():
        start_half(1, lists, coefs, exch, energy, acc, amps, recip)
        near_list(1, lists, coefs, inter, src, acc)


def across_kernel(lists, coefs, inter, xh, recip, acc_in, amps_in, out, acc, amps):
    del acc_in, amps_in
    refs = (lists, coefs, inter, xh, acc)
    across_list_tail(2, *refs)
    step(2 * CAP, SHORT, *refs)
    update_half(0, lists, acc, amps, recip, [out])


def rest_kernel(lists, coefs, inter, exch, energy, src, xh, acc_in, amps_in, recip_in, out_a, out_b, acc, amps, recip):
    del acc_in, amps_in, recip_in

    @pl.when(jnp.logical_not(waits_longer()))
    def _():
        start_half(1, lists, coefs, exch, energy, acc, amps, recip)
        near_list(1, lists, coefs, inter, src, acc)

    refs = (lists, coefs, inter, xh, acc)
    across_list_tail(3, *refs)
    step(3 * CAP, SHORT, *refs)
    update_half(1, lists, acc, amps, recip, [out_a, out_b])


def squares(res):
    s = jnp.sum((res * res).reshape(32, 8, 256), axis=0)
    return s[:, :128] + s[:, 128:]


def near_kernel_2(lists, coefs, inter, exch, energy, x, ia, ib, iha, ihb, amps, acc_in, acc, sq, src):
    del acc_in
    slots = slots_of(0, 8)
    dens = denominators(energy, [coefs[GAP + p] for p in slots], slots)
    total = jnp.zeros((8, 128), F32)
    for q, p in enumerate(slots):
        total = total + squares(lists[LIVE + p].astype(F32) * acc[q])
        acc[q] = exch[p].astype(F32) + dens[q] * amps[q]
    sq[...] = total
    gather(src, x, ia, ib, iha, ihb)
    for half in range(2):
        near_list(half, lists, coefs, inter, src, acc)


def last_kernel(lists, coefs, inter, xh, sq1, acc_in, sums, acc):
    del acc_in
    total = jnp.zeros((8, 128), F32)
    slots = slots_of(0, 8)
    refs = (lists, coefs, inter, xh, acc)
    for half in range(2):
        across_list_tail(2 + half, *refs)
    for half in range(2):
        step((2 + half) * CAP, SHORT, *refs)
        for q in range(4 * half, 4 * half + 4):
            total = total + squares(lists[LIVE + slots[q]].astype(F32) * acc[q])
    row = lax.broadcasted_iota(jnp.int32, sums.shape, 0) & 1
    first = jnp.sum(sq1[...], axis=0, keepdims=True)
    sums[...] = jnp.where(row == 0, first, jnp.sum(total, axis=0, keepdims=True))


def output_kernel(lists, recip, amps, acc, out, buf, sem):
    copies = []
    for q, p in enumerate(slots_of(0, 8)):
        buf[q] = amps[q] - lists[LIVE + p].astype(F32) * acc[q] * recip[q]
        copies.append(pltpu.make_async_copy(buf.at[q], out.at[p], sem.at[q]))
        copies[-1].start()
    for c in copies:
        c.wait()


def on_device(amp_exch, pno_energy, pair_gap, fock, intersection, nbr_slot, nbr_live, pair_live):
    count = lax.axis_size("row")
    v = amp_exch.shape[-1]
    tiles4 = pltpu.VMEM((4, v, v), BF16)
    tiles8 = pltpu.VMEM((8, v, v), F32)
    dma = pltpu.SemaphoreType.DMA
    per_pair = [pltpu.SMEM((8,), F32), pltpu.SMEM((8,), jnp.int32)]
    same_chip = [(i, i ^ 1) for i in range(count) if (i ^ 1) < count]
    other_chip = [(i, i + 1) for i in range(1, count - 1, 2)]
    other_chip += [(j, i) for i, j in other_chip]
    big = [hbm(a) for a in (amp_exch, pno_energy, pair_gap, pair_live, fock, nbr_slot, nbr_live)]

    tiles2 = pltpu.VMEM((2, v, v), BF16)
    slabs = pltpu.VMEM(intersection.shape, BF16)
    intersection = hbm(intersection)
    x0 = pl.pallas_call(
        first_kernel, out_shape=tiles4, in_specs=[AN] * 4, out_specs=VM,
        scratch_shapes=[pltpu.VMEM((4, v, v), BF16), pltpu.VMEM((8, v), F32)] + per_pair + [dma((4,)), dma((3,))],
        compiler_params=params(8), cost_estimate=COST, name="first",
    )(*big[:4])
    xh = lax.ppermute(x0, "row", other_chip)
    i0a, i0b, exch, energy, lists, coefs, inter = pl.pallas_call(
        second_kernel,
        out_shape=[tiles2, tiles2, pltpu.VMEM((8, v, v), BF16), pltpu.VMEM((8, v), F32),
                   pltpu.SMEM((LIVE + 8,), jnp.int32), pltpu.SMEM((GAP + 8,), F32), slabs],
        in_specs=[AN] * 9, out_specs=[VM] * 4 + [SM] * 2 + [VM],
        scratch_shapes=per_pair + [pltpu.SMEM((8, 8), F32)] + [pltpu.SMEM((8, 8), jnp.int32)] * 2
        + [pltpu.SMEM((24,), jnp.int32), pltpu.SMEM((4,), jnp.int32), dma((8,)), dma((6,)), dma((4,))],
        compiler_params=params(8), cost_estimate=COST, name="second",
    )(*big, intersection, x0)

    def swap(*halves):
        return [vmem(lax.ppermute(h, "row", same_chip)) for h in halves]

    meta = (lists, coefs)
    exch, energy = vmem(exch), vmem(energy)
    gathered = pltpu.VMEM((12, v, v), BF16)
    acc, amps, recip, src, inter = pl.pallas_call(
        near_kernel_1, out_shape=[tiles8] * 3 + [gathered, slabs], in_specs=[SM] * 2 + [AN] + [VM] * 8, out_specs=[VM] * 5,
        scratch_shapes=[dma((4,))], input_output_aliases={10: 4},
        compiler_params=params(8), cost_estimate=COST, name="near1",
    )(*meta, intersection, exch, energy, vmem(x0), vmem(i0a), vmem(i0b), *swap(i0a, i0b), vmem(inter))
    inter = vmem(inter)
    x1, acc, amps = pl.pallas_call(
        across_kernel, out_shape=[tiles4, tiles8, tiles8],
        in_specs=[SM] * 2 + [VM] * 5, out_specs=[VM] * 3, input_output_aliases={5: 1, 6: 2},
        compiler_params=params(8), cost_estimate=COST, name="across",
    )(*meta, inter, vmem(xh), vmem(recip), vmem(acc), vmem(amps))
    xh1 = lax.ppermute(x1, "row", other_chip)
    i1a, i1b, acc, amps, recip = pl.pallas_call(
        rest_kernel, out_shape=[tiles2, tiles2] + [tiles8] * 3,
        in_specs=[SM] * 2 + [VM] * 8, out_specs=[VM] * 5, input_output_aliases={7: 2, 8: 3, 9: 4},
        compiler_params=params(8), cost_estimate=COST, name="rest",
    )(*meta, inter, exch, energy, vmem(src), vmem(xh), vmem(acc), vmem(amps), vmem(recip))
    acc, sq = pl.pallas_call(
        near_kernel_2, out_shape=[tiles8, pltpu.VMEM((8, 128), F32)], in_specs=[SM] * 2 + [VM] * 10, out_specs=[VM] * 2,
        scratch_shapes=[gathered], input_output_aliases={11: 0},
        compiler_params=params(8), cost_estimate=COST, name="near2",
    )(*meta, inter, exch, energy, vmem(x1), vmem(i1a), vmem(i1b), *swap(i1a, i1b), vmem(amps), vmem(acc))
    sums, acc = pl.pallas_call(
        last_kernel, out_shape=[pltpu.VMEM((2 * count, 128), F32), tiles8],
        in_specs=[SM] * 2 + [VM] * 4, out_specs=[VM, VM], input_output_aliases={5: 1},
        compiler_params=params(8), cost_estimate=COST, name="last",
    )(*meta, inter, vmem(xh1), vmem(sq), vmem(acc))
    out = pl.pallas_call(
        output_kernel, out_shape=jax.ShapeDtypeStruct((8, v, v), F32), in_specs=[SM] + [VM] * 3, out_specs=AN,
        scratch_shapes=[pltpu.VMEM((8, v, v), F32), dma((8,))],
        compiler_params=params(16), name="output",
        cost_estimate=pl.CostEstimate(flops=10**7, bytes_accessed=10**7, transcendentals=0),
    )(lists, vmem(recip), vmem(amps), vmem(acc))
    sums = lax.all_to_all(sums, "row", 0, 0, tiled=True)
    norms = jnp.sqrt(jnp.sum(sums.reshape(count, 2, 128), axis=(0, 2)) / (amp_exch.shape[0] * count * v * v))
    return out, norms


def solution(mesh):
    whole = P(("grp", "row"))
    return jax.shard_map(
        on_device, mesh=mesh, in_specs=(whole,) * 8, out_specs=(whole, P("grp")), check_vma=False
    )
```

```python
import functools

import jax
import jax.numpy as jnp
from jax import lax
from jax.experimental import pallas as pl
from jax.experimental.pallas import tpu as pltpu
from jax.sharding import PartitionSpec as P

F32 = jnp.float32
BF16 = jnp.bfloat16
VM = pl.BlockSpec(memory_space=pltpu.VMEM)
SM = pl.BlockSpec(memory_space=pltpu.SMEM)
AN = pl.BlockSpec(memory_space=pl.ANY)
CAP = 72
LONG, SHORT = 16, 8
COUNTS, LIVE = 4 * CAP, 4 * CAP + 4
GAP = 4 * CAP
MIB = 1 << 20


def base_slot():
    return lax.rem(lax.axis_index("row"), 2) * 4


def slots_of(first, end):
    base = base_slot()
    return [(q + base) & 7 for q in range(first, end)]


def params(mib, **kw):
    return pltpu.CompilerParams(vmem_limit_bytes=mib * MIB, **kw)


COST = pl.CostEstimate(flops=1000, bytes_accessed=1000, transcendentals=0)


def vmem(x):
    return pltpu.with_memory_space_constraint(x, pltpu.VMEM)


def hbm(x):
    return pltpu.with_memory_space_constraint(x, pltpu.HBM)


def denominators(energy, gaps, slots):
    rows = [energy[pl.ds(p, 1), :] for p in slots]
    fill = [jnp.zeros_like(rows[0])] * (8 - len(rows))
    cols = jnp.transpose(jnp.concatenate(rows + fill, axis=0))
    return [cols[:, i : i + 1] + rows[i] + gaps[i] for i in range(len(slots))]


def start_all(pairs, sems):
    copies = [pltpu.make_async_copy(a, b, sems.at[i]) for i, (a, b) in enumerate(pairs)]
    for c in copies:
        c.start()
    return copies


def first_kernel(exch, energy, gap, live, out, buf, en, gp, lv, sem, sems):
    slots = slots_of(0, 4)
    small = start_all([(energy, en), (gap, gp), (live, lv)], sems)
    tiles = start_all([(exch.at[p], buf.at[i]) for i, p in enumerate(slots)], sem)
    for c in small:
        c.wait()
    dens = denominators(en, [gp[p] for p in slots], slots)
    factors = [-lv[p].astype(F32) / dens[i] for i, p in enumerate(slots)]
    for i in range(4):
        tiles[i].wait()
        out[i] = (buf[i].astype(F32) * factors[i]).astype(BF16)


def second_kernel(
    exch, energy, gap, live, fock, nslot, nlive, inter_hbm, x, out_a, out_b, ex, en, lists, coefs, inter,
    gp, lv, fk, ns, nl, table, ends, sem, sems, slab_sem,
):
    del x
    slots = slots_of(4, 8)
    base = base_slot()
    small = start_all([(energy, en), (gap, gp), (live, lv), (fock, fk), (nslot, ns), (nlive, nl)], sems)
    order = slots + slots_of(0, 4)
    tiles = start_all([(exch.at[p], ex.at[p]) for p in order], sem)
    slabs = start_all([(inter_hbm.at[p], inter.at[p]) for p in order[4:]], slab_sem)
    for c in small:
        c.wait()
    dens = denominators(en, [gp[p] for p in slots], slots)
    for i, p in enumerate(slots):
        tiles[i].wait()
        tile = (-lv[p].astype(F32) * ex[p].astype(F32) / dens[i]).astype(BF16)
        if i < 2:
            out_a[i] = tile
        else:
            out_b[i - 2] = tile

    for s in range(4):
        table[4 + s] = jnp.where(base == 0, (s << 9) | 3, ((8 + s) << 9) | 1)
        table[16 + s] = jnp.where(base == 0, ((8 + s) << 9) | 1, (s << 9) | 3)
    for s in range(8):
        table[8 + s] = (((s + base) & 7) << 9) | lv[s]
    for k in range(4):
        ends[k] = k * CAP

    def entry(i, _):
        q, n = i >> 3, i & 7
        p = (q + base) & 7
        what = table[ns[p, n]]
        which = (what & 2) + (q >> 2)
        pos = ends[which]
        lists[pos] = ((what >> 9) << 9) | (q << 6) | (p << 3) | n
        coefs[pos] = fk[p, n]
        ends[which] = pos + (nl[p, n] & lv[p] & what & 1)
        return 0

    lax.fori_loop(0, 64, entry, 0, unroll=4)
    for k in range(4):
        e = ends[k]
        lists[COUNTS + k] = e - k * CAP
        for u in range(LONG):
            lists[e + u] = base << 3
            coefs[e + u] = 0.0
    for p in range(8):
        lists[LIVE + p] = lv[p]
        coefs[GAP + p] = gp[p]
    for c in tiles[4:] + slabs:
        c.wait()


def step(at, size, lists, coefs, inter, src, acc):
    for u in range(size):
        code = lists[at + u]
        n, p, q, s = code & 7, (code >> 3) & 7, (code >> 6) & 7, code >> 9
        x = inter[p, n]
        h = jnp.dot(x, src[s], preferred_element_type=F32).astype(BF16)
        t = lax.dot_general(h, x, (((1,), (1,)), ((), ())), preferred_element_type=F32)
        acc[q] = acc[q] - coefs[at + u] * t


def steps(at, count, size, *refs):
    def body(i, _):
        step(at + i * size, size, *refs)
        return 0

    lax.fori_loop(0, count, body, 0)


def near_list(which, lists, *refs):
    at, count = which * CAP, lists[COUNTS + which]
    longs = (count + LONG - SHORT - 1) // LONG
    steps(at, longs, LONG, lists, *refs)
    left = jnp.maximum(count - longs * LONG + SHORT - 1, 0)
    steps(at + longs * LONG, left // SHORT, SHORT, lists, *refs)


def across_list_tail(which, lists, *refs):
    more = jnp.maximum(lists[COUNTS + which] - 1, 0) // SHORT
    steps(which * CAP + SHORT, more, SHORT, lists, *refs)


def gather(src, x, ia, ib, iha, ihb):
    src[0:4] = x[...]
    src[4:6] = ia[...]
    src[6:8] = ib[...]
    src[8:10] = iha[...]
    src[10:12] = ihb[...]


def start_half(half, lists, coefs, exch, energy, acc, amps, recip):
    slots = slots_of(4 * half, 4 * half + 4)
    dens = denominators(energy, [coefs[GAP + p] for p in slots], slots)
    for j, p in enumerate(slots):
        q = 4 * half + j
        ex = exch[p].astype(F32)
        a0 = -lists[LIVE + p].astype(F32) * ex / dens[j]
        amps[q] = a0
        recip[q] = 1.0 / dens[j]
        acc[q] = ex + dens[j] * a0


def update_half(half, lists, acc, amps, recip, out):
    each = 4 // len(out)
    for j, p in enumerate(slots_of(4 * half, 4 * half + 4)):
        q = 4 * half + j
        res = lists[LIVE + p].astype(F32) * acc[q]
        a1 = amps[q] - res * recip[q]
        amps[q] = a1
        out[j // each][j % each] = a1.astype(BF16)


def waits_longer():
    return ((lax.axis_index("row") + 1) & 2) != 0


def near_kernel_1(lists, coefs, inter_hbm, exch, energy, x, ia, ib, iha, ihb, inter_in, acc, amps, recip, src, inter, sem):
    del inter_in
    slabs = start_all([(inter_hbm.at[p], inter.at[p]) for p in slots_of(4, 8)], sem)
    gather(src, x, ia, ib, iha, ihb)
    start_half(0, lists, coefs, exch, energy, acc, amps, recip)
    near_list(0, lists, coefs, inter, src, acc)
    for c in slabs:
        c.wait()

    @pl.when(waits_longer())
    def _():
        start_half(1, lists, coefs, exch, energy, acc, amps, recip)
        near_list(1, lists, coefs, inter, src, acc)


def across_kernel(lists, coefs, inter, xh, recip, acc_in, amps_in, out, acc, amps):
    del acc_in, amps_in
    refs = (lists, coefs, inter, xh, acc)
    across_list_tail(2, *refs)
    step(2 * CAP, SHORT, *refs)
    update_half(0, lists, acc, amps, recip, [out])


def rest_kernel(lists, coefs, inter, exch, energy, src, xh, acc_in, amps_in, recip_in, out_a, out_b, acc, amps, recip):
    del acc_in, amps_in, recip_in

    @pl.when(jnp.logical_not(waits_longer()))
    def _():
        start_half(1, lists, coefs, exch, energy, acc, amps, recip)
        near_list(1, lists, coefs, inter, src, acc)

    refs = (lists, coefs, inter, xh, acc)
    across_list_tail(3, *refs)
    step(3 * CAP, SHORT, *refs)
    update_half(1, lists, acc, amps, recip, [out_a, out_b])


def squares(res):
    s = jnp.sum((res * res).reshape(32, 8, 256), axis=0)
    return s[:, :128] + s[:, 128:]


def near_kernel_2(lists, coefs, inter, exch, energy, x, ia, ib, iha, ihb, amps, acc_in, acc, sq, src):
    del acc_in
    slots = slots_of(0, 8)
    dens = denominators(energy, [coefs[GAP + p] for p in slots], slots)
    total = jnp.zeros((8, 128), F32)
    for q, p in enumerate(slots):
        total = total + squares(lists[LIVE + p].astype(F32) * acc[q])
        acc[q] = exch[p].astype(F32) + dens[q] * amps[q]
    sq[...] = total
    gather(src, x, ia, ib, iha, ihb)
    for half in range(2):
        near_list(half, lists, coefs, inter, src, acc)


def last_kernel(lists, coefs, inter, xh, recip, amps, sq1, acc_in, sums, acc):
    del acc_in
    total = jnp.zeros((8, 128), F32)
    slots = slots_of(0, 8)
    refs = (lists, coefs, inter, xh, acc)
    for half in range(2):
        across_list_tail(2 + half, *refs)
    for half in range(2):
        step((2 + half) * CAP, SHORT, *refs)
        for q in range(4 * half, 4 * half + 4):
            res = lists[LIVE + slots[q]].astype(F32) * acc[q]
            total = total + squares(res)
            acc[q] = amps[q] - res * recip[q]
    row = lax.broadcasted_iota(jnp.int32, sums.shape, 0) & 1
    first = jnp.sum(sq1[...], axis=0, keepdims=True)
    sums[...] = jnp.where(row == 0, first, jnp.sum(total, axis=0, keepdims=True))


def output_kernel(tiles, out, sem):
    for c in start_all([(tiles.at[q], out.at[p]) for q, p in enumerate(slots_of(0, 8))], sem):
        c.wait()


def on_device(amp_exch, pno_energy, pair_gap, fock, intersection, nbr_slot, nbr_live, pair_live):
    count = lax.axis_size("row")
    v = amp_exch.shape[-1]
    tiles4 = pltpu.VMEM((4, v, v), BF16)
    tiles8 = pltpu.VMEM((8, v, v), F32)
    dma = pltpu.SemaphoreType.DMA
    per_pair = [pltpu.SMEM((8,), F32), pltpu.SMEM((8,), jnp.int32)]
    same_chip = [(i, i ^ 1) for i in range(count) if (i ^ 1) < count]
    other_chip = [(i, i + 1) for i in range(1, count - 1, 2)]
    other_chip += [(j, i) for i, j in other_chip]
    big = [hbm(a) for a in (amp_exch, pno_energy, pair_gap, pair_live, fock, nbr_slot, nbr_live)]

    tiles2 = pltpu.VMEM((2, v, v), BF16)
    slabs = pltpu.VMEM(intersection.shape, BF16)
    intersection = hbm(intersection)
    x0 = pl.pallas_call(
        first_kernel, out_shape=tiles4, in_specs=[AN] * 4, out_specs=VM,
        scratch_shapes=[pltpu.VMEM((4, v, v), BF16), pltpu.VMEM((8, v), F32)] + per_pair + [dma((4,)), dma((3,))],
        compiler_params=params(8), cost_estimate=COST, name="first",
    )(*big[:4])
    xh = lax.ppermute(x0, "row", other_chip)
    i0a, i0b, exch, energy, lists, coefs, inter = pl.pallas_call(
        second_kernel,
        out_shape=[tiles2, tiles2, pltpu.VMEM((8, v, v), BF16), pltpu.VMEM((8, v), F32),
                   pltpu.SMEM((LIVE + 8,), jnp.int32), pltpu.SMEM((GAP + 8,), F32), slabs],
        in_specs=[AN] * 9, out_specs=[VM] * 4 + [SM] * 2 + [VM],
        scratch_shapes=per_pair + [pltpu.SMEM((8, 8), F32)] + [pltpu.SMEM((8, 8), jnp.int32)] * 2
        + [pltpu.SMEM((24,), jnp.int32), pltpu.SMEM((4,), jnp.int32), dma((8,)), dma((6,)), dma((4,))],
        compiler_params=params(8), cost_estimate=COST, name="second",
    )(*big, intersection, x0)

    def swap(*halves):
        return [vmem(lax.ppermute(h, "row", same_chip)) for h in halves]

    meta = (lists, coefs)
    exch, energy = vmem(exch), vmem(energy)
    gathered = pltpu.VMEM((12, v, v), BF16)
    acc, amps, recip, src, inter = pl.pallas_call(
        near_kernel_1, out_shape=[tiles8] * 3 + [gathered, slabs], in_specs=[SM] * 2 + [AN] + [VM] * 8, out_specs=[VM] * 5,
        scratch_shapes=[dma((4,))], input_output_aliases={10: 4},
        compiler_params=params(8), cost_estimate=COST, name="near1",
    )(*meta, intersection, exch, energy, vmem(x0), vmem(i0a), vmem(i0b), *swap(i0a, i0b), vmem(inter))
    inter = vmem(inter)
    x1, acc, amps = pl.pallas_call(
        across_kernel, out_shape=[tiles4, tiles8, tiles8],
        in_specs=[SM] * 2 + [VM] * 5, out_specs=[VM] * 3, input_output_aliases={5: 1, 6: 2},
        compiler_params=params(8), cost_estimate=COST, name="across",
    )(*meta, inter, vmem(xh), vmem(recip), vmem(acc), vmem(amps))
    xh1 = lax.ppermute(x1, "row", other_chip)
    i1a, i1b, acc, amps, recip = pl.pallas_call(
        rest_kernel, out_shape=[tiles2, tiles2] + [tiles8] * 3,
        in_specs=[SM] * 2 + [VM] * 8, out_specs=[VM] * 5, input_output_aliases={7: 2, 8: 3, 9: 4},
        compiler_params=params(8), cost_estimate=COST, name="rest",
    )(*meta, inter, exch, energy, vmem(src), vmem(xh), vmem(acc), vmem(amps), vmem(recip))
    acc, sq = pl.pallas_call(
        near_kernel_2, out_shape=[tiles8, pltpu.VMEM((8, 128), F32)], in_specs=[SM] * 2 + [VM] * 10, out_specs=[VM] * 2,
        scratch_shapes=[gathered], input_output_aliases={11: 0},
        compiler_params=params(8), cost_estimate=COST, name="near2",
    )(*meta, inter, exch, energy, vmem(x1), vmem(i1a), vmem(i1b), *swap(i1a, i1b), vmem(amps), vmem(acc))
    sums, acc = pl.pallas_call(
        last_kernel, out_shape=[pltpu.VMEM((2 * count, 128), F32), tiles8],
        in_specs=[SM] * 2 + [VM] * 6, out_specs=[VM, VM], input_output_aliases={7: 1},
        compiler_params=params(8), cost_estimate=COST, name="last",
    )(*meta, inter, vmem(xh1), vmem(recip), vmem(amps), vmem(sq), vmem(acc))
    out = pl.pallas_call(
        output_kernel, out_shape=jax.ShapeDtypeStruct((8, v, v), F32), in_specs=[VM], out_specs=AN,
        scratch_shapes=[dma((8,))], compiler_params=params(4), name="output",
        cost_estimate=pl.CostEstimate(flops=10**6, bytes_accessed=10**7, transcendentals=0),
    )(vmem(acc))
    sums = lax.all_to_all(sums, "row", 0, 0, tiled=True)
    norms = jnp.sqrt(jnp.sum(sums.reshape(count, 2, 128), axis=(0, 2)) / (amp_exch.shape[0] * count * v * v))
    return out, norms


def solution(mesh):
    whole = P(("grp", "row"))
    return jax.shard_map(
        on_device, mesh=mesh, in_specs=(whole,) * 8, out_specs=(whole, P("grp")), check_vma=False
    )
```

```python
import functools

import jax
import jax.numpy as jnp
from jax import lax
from jax.experimental import pallas as pl
from jax.experimental.pallas import tpu as pltpu
from jax.sharding import PartitionSpec as P

F32 = jnp.float32
BF16 = jnp.bfloat16
VM = pl.BlockSpec(memory_space=pltpu.VMEM)
SM = pl.BlockSpec(memory_space=pltpu.SMEM)
AN = pl.BlockSpec(memory_space=pl.ANY)
CAP = 72
LONG, SHORT = 16, 8
COUNTS, LIVE = 4 * CAP, 4 * CAP + 4
GAP = 4 * CAP
MIB = 1 << 20


def base_slot():
    return lax.rem(lax.axis_index("row"), 2) * 4


def slots_of(first, end):
    base = base_slot()
    return [(q + base) & 7 for q in range(first, end)]


def params(mib, **kw):
    return pltpu.CompilerParams(vmem_limit_bytes=mib * MIB, **kw)


COST = pl.CostEstimate(flops=1000, bytes_accessed=1000, transcendentals=0)


def vmem(x):
    return pltpu.with_memory_space_constraint(x, pltpu.VMEM)


def hbm(x):
    return pltpu.with_memory_space_constraint(x, pltpu.HBM)


def denominators(energy, gaps, slots):
    rows = [energy[pl.ds(p, 1), :] for p in slots]
    fill = [jnp.zeros_like(rows[0])] * (8 - len(rows))
    cols = jnp.transpose(jnp.concatenate(rows + fill, axis=0))
    return [cols[:, i : i + 1] + rows[i] + gaps[i] for i in range(len(slots))]


def start_all(pairs, sems):
    copies = [pltpu.make_async_copy(a, b, sems.at[i]) for i, (a, b) in enumerate(pairs)]
    for c in copies:
        c.start()
    return copies


def first_kernel(exch, energy, gap, live, out, buf, en, gp, lv, sem, sems):
    slots = slots_of(0, 4)
    small = start_all([(energy, en), (gap, gp), (live, lv)], sems)
    tiles = start_all([(exch.at[p], buf.at[i]) for i, p in enumerate(slots)], sem)
    for c in small:
        c.wait()
    dens = denominators(en, [gp[p] for p in slots], slots)
    factors = [-lv[p].astype(F32) / dens[i] for i, p in enumerate(slots)]
    for i in range(4):
        tiles[i].wait()
        out[i] = (buf[i].astype(F32) * factors[i]).astype(BF16)


def second_kernel(
    exch, energy, gap, live, fock, nslot, nlive, inter_hbm, x, out_a, out_b, ex, en, lists, coefs, inter,
    gp, lv, fk, ns, nl, table, ends, sem, sems, slab_sem,
):
    del x
    slots = slots_of(4, 8)
    base = base_slot()
    small = start_all([(energy, en), (gap, gp), (live, lv), (fock, fk), (nslot, ns), (nlive, nl)], sems)
    order = slots + slots_of(0, 4)
    tiles = start_all([(exch.at[p], ex.at[p]) for p in order], sem)
    slabs = start_all([(inter_hbm.at[p], inter.at[p]) for p in order[4:]], slab_sem)
    for c in small:
        c.wait()
    dens = denominators(en, [gp[p] for p in slots], slots)
    for i, p in enumerate(slots):
        tiles[i].wait()
        tile = (-lv[p].astype(F32) * ex[p].astype(F32) / dens[i]).astype(BF16)
        if i < 2:
            out_a[i] = tile
        else:
            out_b[i - 2] = tile

    for s in range(4):
        table[4 + s] = jnp.where(base == 0, (s << 9) | 3, ((8 + s) << 9) | 1)
        table[16 + s] = jnp.where(base == 0, ((8 + s) << 9) | 1, (s << 9) | 3)
    for s in range(8):
        table[8 + s] = (((s + base) & 7) << 9) | lv[s]
    for k in range(4):
        ends[k] = k * CAP

    def entry(i, _):
        q, n = i >> 3, i & 7
        p = (q + base) & 7
        what = table[ns[p, n]]
        which = (what & 2) + (q >> 2)
        pos = ends[which]
        lists[pos] = ((what >> 9) << 9) | (q << 6) | (p << 3) | n
        coefs[pos] = fk[p, n]
        ends[which] = pos + (nl[p, n] & lv[p] & what & 1)
        return 0

    lax.fori_loop(0, 64, entry, 0, unroll=4)
    for k in range(4):
        e = ends[k]
        lists[COUNTS + k] = e - k * CAP
        for u in range(LONG):
            lists[e + u] = base << 3
            coefs[e + u] = 0.0
    for p in range(8):
        lists[LIVE + p] = lv[p]
        coefs[GAP + p] = gp[p]
    for c in tiles[4:] + slabs:
        c.wait()


def step(at, size, lists, coefs, inter, src, acc):
    for u in range(size):
        code = lists[at + u]
        n, p, q, s = code & 7, (code >> 3) & 7, (code >> 6) & 7, code >> 9
        x = inter[p, n]
        h = jnp.dot(x, src[s], preferred_element_type=F32).astype(BF16)
        t = lax.dot_general(h, x, (((1,), (1,)), ((), ())), preferred_element_type=F32)
        acc[q] = acc[q] - coefs[at + u] * t


def steps(at, count, size, *refs):
    def body(i, _):
        step(at + i * size, size, *refs)
        return 0

    lax.fori_loop(0, count, body, 0)


def near_list(which, lists, *refs):
    at, count = which * CAP, lists[COUNTS + which]
    longs = (count + LONG - SHORT - 1) // LONG
    steps(at, longs, LONG, lists, *refs)
    left = jnp.maximum(count - longs * LONG + SHORT - 1, 0)
    steps(at + longs * LONG, left // SHORT, SHORT, lists, *refs)


def across_list_tail(which, lists, *refs):
    more = jnp.maximum(lists[COUNTS + which] - 1, 0) // SHORT
    steps(which * CAP + SHORT, more, SHORT, lists, *refs)


def gather(src, x, ia, ib, iha, ihb):
    src[0:4] = x[...]
    src[4:6] = ia[...]
    src[6:8] = ib[...]
    src[8:10] = iha[...]
    src[10:12] = ihb[...]


def start_half(half, lists, coefs, exch, energy, acc, amps, recip):
    slots = slots_of(4 * half, 4 * half + 4)
    dens = denominators(energy, [coefs[GAP + p] for p in slots], slots)
    for j, p in enumerate(slots):
        q = 4 * half + j
        ex = exch[p].astype(F32)
        a0 = -lists[LIVE + p].astype(F32) * ex / dens[j]
        amps[q] = a0
        recip[q] = 1.0 / dens[j]
        acc[q] = ex + dens[j] * a0


def update_half(half, lists, acc, amps, recip, out):
    each = 4 // len(out)
    for j, p in enumerate(slots_of(4 * half, 4 * half + 4)):
        q = 4 * half + j
        res = lists[LIVE + p].astype(F32) * acc[q]
        a1 = amps[q] - res * recip[q]
        amps[q] = a1
        out[j // each][j % each] = a1.astype(BF16)


def waits_longer():
    return ((lax.axis_index("row") + 1) & 2) != 0


def near_kernel_1(lists, coefs, inter_hbm, exch, energy, x, ia, ib, iha, ihb, inter_in, acc, amps, recip, src, inter, sem):
    del inter_in
    slabs = start_all([(inter_hbm.at[p], inter.at[p]) for p in slots_of(4, 8)], sem)
    gather(src, x, ia, ib, iha, ihb)
    start_half(0, lists, coefs, exch, energy, acc, amps, recip)
    near_list(0, lists, coefs, inter, src, acc)
    for c in slabs:
        c.wait()

    @pl.when(waits_longer())
    def _():
        start_half(1, lists, coefs, exch, energy, acc, amps, recip)
        near_list(1, lists, coefs, inter, src, acc)


def across_kernel(lists, coefs, inter, xh, recip, acc_in, amps_in, out, acc, amps):
    del acc_in, amps_in
    refs = (lists, coefs, inter, xh, acc)
    across_list_tail(2, *refs)
    step(2 * CAP, SHORT, *refs)
    update_half(0, lists, acc, amps, recip, [out])


def rest_kernel(lists, coefs, inter, exch, energy, src, xh, acc_in, amps_in, recip_in, out_a, out_b, acc, amps, recip):
    del acc_in, amps_in, recip_in

    @pl.when(jnp.logical_not(waits_longer()))
    def _():
        start_half(1, lists, coefs, exch, energy, acc, amps, recip)
        near_list(1, lists, coefs, inter, src, acc)

    refs = (lists, coefs, inter, xh, acc)
    across_list_tail(3, *refs)
    step(3 * CAP, SHORT, *refs)
    update_half(1, lists, acc, amps, recip, [out_a, out_b])


def squares(res):
    s = jnp.sum((res * res).reshape(32, 8, 256), axis=0)
    return s[:, :128] + s[:, 128:]


def near_kernel_2(lists, coefs, inter, exch, energy, x, ia, ib, iha, ihb, amps, acc_in, acc, sq, src):
    del acc_in
    slots = slots_of(0, 8)
    dens = denominators(energy, [coefs[GAP + p] for p in slots], slots)
    total = jnp.zeros((8, 128), F32)
    for q, p in enumerate(slots):
        total = total + squares(lists[LIVE + p].astype(F32) * acc[q])
        acc[q] = exch[p].astype(F32) + dens[q] * amps[q]
    sq[...] = total
    gather(src, x, ia, ib, iha, ihb)
    for half in range(2):
        near_list(half, lists, coefs, inter, src, acc)


def last_kernel(lists, coefs, inter, xh, sq1, acc_in, sums, acc):
    del acc_in
    total = jnp.zeros((8, 128), F32)
    slots = slots_of(0, 8)
    refs = (lists, coefs, inter, xh, acc)

    @pl.when(jnp.maximum(lists[COUNTS + 2], lists[COUNTS + 3]) > SHORT)
    def _():
        for half in range(2):
            across_list_tail(2 + half, *refs)

    for half in range(2):
        step((2 + half) * CAP, SHORT, *refs)
        for q in range(4 * half, 4 * half + 4):
            total = total + squares(lists[LIVE + slots[q]].astype(F32) * acc[q])
    row = lax.broadcasted_iota(jnp.int32, sums.shape, 0) & 1
    first = jnp.sum(sq1[...], axis=0, keepdims=True)
    sums[...] = jnp.where(row == 0, first, jnp.sum(total, axis=0, keepdims=True))


def output_kernel(lists, recip, amps, acc, out, buf, sem):
    copies = []
    for q, p in enumerate(slots_of(0, 8)):
        buf[q] = amps[q] - lists[LIVE + p].astype(F32) * acc[q] * recip[q]
        copies.append(pltpu.make_async_copy(buf.at[q], out.at[p], sem.at[q]))
        copies[-1].start()
    for c in copies:
        c.wait()


def on_device(amp_exch, pno_energy, pair_gap, fock, intersection, nbr_slot, nbr_live, pair_live):
    count = lax.axis_size("row")
    v = amp_exch.shape[-1]
    tiles4 = pltpu.VMEM((4, v, v), BF16)
    tiles8 = pltpu.VMEM((8, v, v), F32)
    dma = pltpu.SemaphoreType.DMA
    per_pair = [pltpu.SMEM((8,), F32), pltpu.SMEM((8,), jnp.int32)]
    same_chip = [(i, i ^ 1) for i in range(count) if (i ^ 1) < count]
    other_chip = [(i, i + 1) for i in range(1, count - 1, 2)]
    other_chip += [(j, i) for i, j in other_chip]
    big = [hbm(a) for a in (amp_exch, pno_energy, pair_gap, pair_live, fock, nbr_slot, nbr_live)]

    tiles2 = pltpu.VMEM((2, v, v), BF16)
    slabs = pltpu.VMEM(intersection.shape, BF16)
    intersection = hbm(intersection)
    x0 = pl.pallas_call(
        first_kernel, out_shape=tiles4, in_specs=[AN] * 4, out_specs=VM,
        scratch_shapes=[pltpu.VMEM((4, v, v), BF16), pltpu.VMEM((8, v), F32)] + per_pair + [dma((4,)), dma((3,))],
        compiler_params=params(8), cost_estimate=COST, name="first",
    )(*big[:4])
    xh = lax.ppermute(x0, "row", other_chip)
    i0a, i0b, exch, energy, lists, coefs, inter = pl.pallas_call(
        second_kernel,
        out_shape=[tiles2, tiles2, pltpu.VMEM((8, v, v), BF16), pltpu.VMEM((8, v), F32),
                   pltpu.SMEM((LIVE + 8,), jnp.int32), pltpu.SMEM((GAP + 8,), F32), slabs],
        in_specs=[AN] * 9, out_specs=[VM] * 4 + [SM] * 2 + [VM],
        scratch_shapes=per_pair + [pltpu.SMEM((8, 8), F32)] + [pltpu.SMEM((8, 8), jnp.int32)] * 2
        + [pltpu.SMEM((24,), jnp.int32), pltpu.SMEM((4,), jnp.int32), dma((8,)), dma((6,)), dma((4,))],
        compiler_params=params(8), cost_estimate=COST, name="second",
    )(*big, intersection, x0)

    def swap(*halves):
        return [vmem(lax.ppermute(h, "row", same_chip)) for h in halves]

    meta = (lists, coefs)
    exch, energy = vmem(exch), vmem(energy)
    gathered = pltpu.VMEM((12, v, v), BF16)
    acc, amps, recip, src, inter = pl.pallas_call(
        near_kernel_1, out_shape=[tiles8] * 3 + [gathered, slabs], in_specs=[SM] * 2 + [AN] + [VM] * 8, out_specs=[VM] * 5,
        scratch_shapes=[dma((4,))], input_output_aliases={10: 4},
        compiler_params=params(8), cost_estimate=COST, name="near1",
    )(*meta, intersection, exch, energy, vmem(x0), vmem(i0a), vmem(i0b), *swap(i0a, i0b), vmem(inter))
    inter = vmem(inter)
    x1, acc, amps = pl.pallas_call(
        across_kernel, out_shape=[tiles4, tiles8, tiles8],
        in_specs=[SM] * 2 + [VM] * 5, out_specs=[VM] * 3, input_output_aliases={5: 1, 6: 2},
        compiler_params=params(8), cost_estimate=COST, name="across",
    )(*meta, inter, vmem(xh), vmem(recip), vmem(acc), vmem(amps))
    xh1 = lax.ppermute(x1, "row", other_chip)
    i1a, i1b, acc, amps, recip = pl.pallas_call(
        rest_kernel, out_shape=[tiles2, tiles2] + [tiles8] * 3,
        in_specs=[SM] * 2 + [VM] * 8, out_specs=[VM] * 5, input_output_aliases={7: 2, 8: 3, 9: 4},
        compiler_params=params(8), cost_estimate=COST, name="rest",
    )(*meta, inter, exch, energy, vmem(src), vmem(xh), vmem(acc), vmem(amps), vmem(recip))
    acc, sq = pl.pallas_call(
        near_kernel_2, out_shape=[tiles8, pltpu.VMEM((8, 128), F32)], in_specs=[SM] * 2 + [VM] * 10, out_specs=[VM] * 2,
        scratch_shapes=[gathered], input_output_aliases={11: 0},
        compiler_params=params(8), cost_estimate=COST, name="near2",
    )(*meta, inter, exch, energy, vmem(x1), vmem(i1a), vmem(i1b), *swap(i1a, i1b), vmem(amps), vmem(acc))
    sums, acc = pl.pallas_call(
        last_kernel, out_shape=[pltpu.VMEM((2 * count, 128), F32), tiles8],
        in_specs=[SM] * 2 + [VM] * 4, out_specs=[VM, VM], input_output_aliases={5: 1},
        compiler_params=params(8), cost_estimate=COST, name="last",
    )(*meta, inter, vmem(xh1), vmem(sq), vmem(acc))
    out = pl.pallas_call(
        output_kernel, out_shape=jax.ShapeDtypeStruct((8, v, v), F32), in_specs=[SM] + [VM] * 3, out_specs=AN,
        scratch_shapes=[pltpu.VMEM((8, v, v), F32), dma((8,))],
        compiler_params=params(16), name="output",
        cost_estimate=pl.CostEstimate(flops=10**7, bytes_accessed=10**7, transcendentals=0),
    )(lists, vmem(recip), vmem(amps), vmem(acc))
    sums = lax.all_to_all(sums, "row", 0, 0, tiled=True)
    sums = sum(sums[2 * i : 2 * i + 2] for i in range(count))
    norms = jnp.sqrt(jnp.sum(sums, axis=1) / (amp_exch.shape[0] * count * v * v))
    return out, norms


def solution(mesh):
    whole = P(("grp", "row"))
    return jax.shard_map(
        on_device, mesh=mesh, in_specs=(whole,) * 8, out_specs=(whole, P("grp")), check_vma=False
    )
```

```python
import functools

import jax
import jax.numpy as jnp
from jax import lax
from jax.experimental import pallas as pl
from jax.experimental.pallas import tpu as pltpu
from jax.sharding import PartitionSpec as P

F32 = jnp.float32
BF16 = jnp.bfloat16
VM = pl.BlockSpec(memory_space=pltpu.VMEM)
SM = pl.BlockSpec(memory_space=pltpu.SMEM)
AN = pl.BlockSpec(memory_space=pl.ANY)
CAP = 72
LONG, SHORT = 16, 8
COUNTS, LIVE = 4 * CAP, 4 * CAP + 4
GAP = 4 * CAP
MIB = 1 << 20


def base_slot():
    return lax.rem(lax.axis_index("row"), 2) * 4


def slots_of(first, end):
    base = base_slot()
    return [(q + base) & 7 for q in range(first, end)]


def params(mib, **kw):
    return pltpu.CompilerParams(vmem_limit_bytes=mib * MIB, **kw)


COST = pl.CostEstimate(flops=1000, bytes_accessed=1000, transcendentals=0)


def vmem(x):
    return pltpu.with_memory_space_constraint(x, pltpu.VMEM)


def hbm(x):
    return pltpu.with_memory_space_constraint(x, pltpu.HBM)


def denominators(energy, gaps, slots):
    rows = [energy[pl.ds(p, 1), :] for p in slots]
    fill = [jnp.zeros_like(rows[0])] * (8 - len(rows))
    cols = jnp.transpose(jnp.concatenate(rows + fill, axis=0))
    return [cols[:, i : i + 1] + rows[i] + gaps[i] for i in range(len(slots))]


def start_all(pairs, sems):
    copies = [pltpu.make_async_copy(a, b, sems.at[i]) for i, (a, b) in enumerate(pairs)]
    for c in copies:
        c.start()
    return copies


def first_kernel(exch, energy, gap, live, out, buf, en, gp, lv, sem, sems):
    slots = slots_of(0, 4)
    small = start_all([(energy, en), (gap, gp), (live, lv)], sems)
    tiles = start_all([(exch.at[p], buf.at[i]) for i, p in enumerate(slots)], sem)
    for c in small:
        c.wait()
    dens = denominators(en, [gp[p] for p in slots], slots)
    factors = []
    for i, p in enumerate(slots):
        guess = pl.reciprocal(dens[i], approx=True)
        guess = guess * (2.0 - dens[i] * guess)
        factors.append(-lv[p].astype(F32) * (guess * (2.0 - dens[i] * guess)))
    for i in range(4):
        tiles[i].wait()
        out[i] = (buf[i].astype(F32) * factors[i]).astype(BF16)


def second_kernel(
    exch, energy, gap, live, fock, nslot, nlive, inter_hbm, x, out_a, out_b, ex, en, lists, coefs, inter,
    gp, lv, fk, ns, nl, table, ends, sem, sems, slab_sem,
):
    del x
    slots = slots_of(4, 8)
    base = base_slot()
    small = start_all([(energy, en), (gap, gp), (live, lv), (fock, fk), (nslot, ns), (nlive, nl)], sems)
    order = slots + slots_of(0, 4)
    tiles = start_all([(exch.at[p], ex.at[p]) for p in order], sem)
    slabs = start_all([(inter_hbm.at[p], inter.at[p]) for p in order[4:]], slab_sem)
    for c in small:
        c.wait()
    dens = denominators(en, [gp[p] for p in slots], slots)
    for i, p in enumerate(slots):
        tiles[i].wait()
        tile = (-lv[p].astype(F32) * ex[p].astype(F32) / dens[i]).astype(BF16)
        if i < 2:
            out_a[i] = tile
        else:
            out_b[i - 2] = tile

    for s in range(4):
        table[4 + s] = jnp.where(base == 0, (s << 9) | 3, ((8 + s) << 9) | 1)
        table[16 + s] = jnp.where(base == 0, ((8 + s) << 9) | 1, (s << 9) | 3)
    for s in range(8):
        table[8 + s] = (((s + base) & 7) << 9) | lv[s]
    for k in range(4):
        ends[k] = k * CAP

    def entry(i, _):
        q, n = i >> 3, i & 7
        p = (q + base) & 7
        what = table[ns[p, n]]
        which = (what & 2) + (q >> 2)
        pos = ends[which]
        lists[pos] = ((what >> 9) << 9) | (q << 6) | (p << 3) | n
        coefs[pos] = fk[p, n]
        ends[which] = pos + (nl[p, n] & lv[p] & what & 1)
        return 0

    lax.fori_loop(0, 64, entry, 0, unroll=4)
    for k in range(4):
        e = ends[k]
        lists[COUNTS + k] = e - k * CAP
        for u in range(LONG):
            lists[e + u] = base << 3
            coefs[e + u] = 0.0
    for p in range(8):
        lists[LIVE + p] = lv[p]
        coefs[GAP + p] = gp[p]
    for c in tiles[4:] + slabs:
        c.wait()


def step(at, size, lists, coefs, inter, src, acc):
    for u in range(size):
        code = lists[at + u]
        n, p, q, s = code & 7, (code >> 3) & 7, (code >> 6) & 7, code >> 9
        x = inter[p, n]
        h = jnp.dot(x, src[s], preferred_element_type=F32).astype(BF16)
        t = lax.dot_general(h, x, (((1,), (1,)), ((), ())), preferred_element_type=F32)
        acc[q] = acc[q] - coefs[at + u] * t


def steps(at, count, size, *refs):
    def body(i, _):
        step(at + i * size, size, *refs)
        return 0

    lax.fori_loop(0, count, body, 0)


def near_list(which, lists, *refs):
    at, count = which * CAP, lists[COUNTS + which]
    longs = (count + LONG - SHORT - 1) // LONG
    steps(at, longs, LONG, lists, *refs)
    left = jnp.maximum(count - longs * LONG + SHORT - 1, 0)
    steps(at + longs * LONG, left // SHORT, SHORT, lists, *refs)


def across_list_tail(which, lists, *refs):
    more = jnp.maximum(lists[COUNTS + which] - 1, 0) // SHORT
    steps(which * CAP + SHORT, more, SHORT, lists, *refs)


def gather(src, x, ia, ib, iha, ihb):
    src[0:4] = x[...]
    src[4:6] = ia[...]
    src[6:8] = ib[...]
    src[8:10] = iha[...]
    src[10:12] = ihb[...]


def start_half(half, lists, coefs, exch, energy, acc, amps, recip):
    slots = slots_of(4 * half, 4 * half + 4)
    dens = denominators(energy, [coefs[GAP + p] for p in slots], slots)
    for j, p in enumerate(slots):
        q = 4 * half + j
        ex = exch[p].astype(F32)
        a0 = -lists[LIVE + p].astype(F32) * ex / dens[j]
        amps[q] = a0
        recip[q] = 1.0 / dens[j]
        acc[q] = ex + dens[j] * a0


def update_half(half, lists, acc, amps, recip, out):
    each = 4 // len(out)
    for j, p in enumerate(slots_of(4 * half, 4 * half + 4)):
        q = 4 * half + j
        res = lists[LIVE + p].astype(F32) * acc[q]
        a1 = amps[q] - res * recip[q]
        amps[q] = a1
        out[j // each][j % each] = a1.astype(BF16)


def waits_longer():
    return ((lax.axis_index("row") + 1) & 2) != 0


def near_kernel_1(lists, coefs, inter_hbm, exch, energy, x, ia, ib, iha, ihb, inter_in, acc, amps, recip, src, inter, sem):
    del inter_in
    slabs = start_all([(inter_hbm.at[p], inter.at[p]) for p in slots_of(4, 8)], sem)
    gather(src, x, ia, ib, iha, ihb)
    start_half(0, lists, coefs, exch, energy, acc, amps, recip)
    near_list(0, lists, coefs, inter, src, acc)
    for c in slabs:
        c.wait()

    @pl.when(waits_longer())
    def _():
        start_half(1, lists, coefs, exch, energy, acc, amps, recip)
        near_list(1, lists, coefs, inter, src, acc)


def across_kernel(lists, coefs, inter, xh, recip, acc_in, amps_in, out, acc, amps):
    del acc_in, amps_in
    refs = (lists, coefs, inter, xh, acc)
    across_list_tail(2, *refs)
    step(2 * CAP, SHORT, *refs)
    update_half(0, lists, acc, amps, recip, [out])


def rest_kernel(lists, coefs, inter, exch, energy, src, xh, acc_in, amps_in, recip_in, out_a, out_b, acc, amps, recip):
    del acc_in, amps_in, recip_in

    @pl.when(jnp.logical_not(waits_longer()))
    def _():
        start_half(1, lists, coefs, exch, energy, acc, amps, recip)
        near_list(1, lists, coefs, inter, src, acc)

    refs = (lists, coefs, inter, xh, acc)
    across_list_tail(3, *refs)
    step(3 * CAP, SHORT, *refs)
    update_half(1, lists, acc, amps, recip, [out_a, out_b])


def squares(res):
    s = jnp.sum((res * res).reshape(32, 8, 256), axis=0)
    return s[:, :128] + s[:, 128:]


def near_kernel_2(lists, coefs, inter, exch, energy, x, ia, ib, iha, ihb, amps, acc_in, acc, sq, src):
    del acc_in
    slots = slots_of(0, 8)
    dens = denominators(energy, [coefs[GAP + p] for p in slots], slots)
    total = jnp.zeros((8, 128), F32)
    for q, p in enumerate(slots):
        total = total + squares(lists[LIVE + p].astype(F32) * acc[q])
        acc[q] = exch[p].astype(F32) + dens[q] * amps[q]
    sq[...] = total
    gather(src, x, ia, ib, iha, ihb)
    for half in range(2):
        near_list(half, lists, coefs, inter, src, acc)


def last_kernel(lists, coefs, inter, xh, sq1, acc_in, sums, acc):
    del acc_in
    total = jnp.zeros((8, 128), F32)
    slots = slots_of(0, 8)
    refs = (lists, coefs, inter, xh, acc)
    for half in range(2):
        across_list_tail(2 + half, *refs)
    for half in range(2):
        step((2 + half) * CAP, SHORT, *refs)
        for q in range(4 * half, 4 * half + 4):
            total = total + squares(lists[LIVE + slots[q]].astype(F32) * acc[q])
    row = lax.broadcasted_iota(jnp.int32, sums.shape, 0) & 1
    first = jnp.sum(sq1[...], axis=0, keepdims=True)
    sums[...] = jnp.where(row == 0, first, jnp.sum(total, axis=0, keepdims=True))


def output_kernel(lists, recip, amps, acc, out, buf, sem):
    copies = []
    for q, p in enumerate(slots_of(0, 8)):
        buf[q] = amps[q] - lists[LIVE + p].astype(F32) * acc[q] * recip[q]
        copies.append(pltpu.make_async_copy(buf.at[q], out.at[p], sem.at[q]))
        copies[-1].start()
    for c in copies:
        c.wait()


def on_device(amp_exch, pno_energy, pair_gap, fock, intersection, nbr_slot, nbr_live, pair_live):
    count = lax.axis_size("row")
    v = amp_exch.shape[-1]
    tiles4 = pltpu.VMEM((4, v, v), BF16)
    tiles8 = pltpu.VMEM((8, v, v), F32)
    dma = pltpu.SemaphoreType.DMA
    per_pair = [pltpu.SMEM((8,), F32), pltpu.SMEM((8,), jnp.int32)]
    same_chip = [(i, i ^ 1) for i in range(count) if (i ^ 1) < count]
    other_chip = [(i, i + 1) for i in range(1, count - 1, 2)]
    other_chip += [(j, i) for i, j in other_chip]
    big = [hbm(a) for a in (amp_exch, pno_energy, pair_gap, pair_live, fock, nbr_slot, nbr_live)]

    tiles2 = pltpu.VMEM((2, v, v), BF16)
    slabs = pltpu.VMEM(intersection.shape, BF16)
    intersection = hbm(intersection)
    x0 = pl.pallas_call(
        first_kernel, out_shape=tiles4, in_specs=[AN] * 4, out_specs=VM,
        scratch_shapes=[pltpu.VMEM((4, v, v), BF16), pltpu.VMEM((8, v), F32)] + per_pair + [dma((4,)), dma((3,))],
        compiler_params=params(8), cost_estimate=COST, name="first",
    )(*big[:4])
    xh = lax.ppermute(x0, "row", other_chip)
    i0a, i0b, exch, energy, lists, coefs, inter = pl.pallas_call(
        second_kernel,
        out_shape=[tiles2, tiles2, pltpu.VMEM((8, v, v), BF16), pltpu.VMEM((8, v), F32),
                   pltpu.SMEM((LIVE + 8,), jnp.int32), pltpu.SMEM((GAP + 8,), F32), slabs],
        in_specs=[AN] * 9, out_specs=[VM] * 4 + [SM] * 2 + [VM],
        scratch_shapes=per_pair + [pltpu.SMEM((8, 8), F32)] + [pltpu.SMEM((8, 8), jnp.int32)] * 2
        + [pltpu.SMEM((24,), jnp.int32), pltpu.SMEM((4,), jnp.int32), dma((8,)), dma((6,)), dma((4,))],
        compiler_params=params(8), cost_estimate=COST, name="second",
    )(*big, intersection, x0)

    def swap(*halves):
        return [vmem(lax.ppermute(h, "row", same_chip)) for h in halves]

    meta = (lists, coefs)
    exch, energy = vmem(exch), vmem(energy)
    gathered = pltpu.VMEM((12, v, v), BF16)
    acc, amps, recip, src, inter = pl.pallas_call(
        near_kernel_1, out_shape=[tiles8] * 3 + [gathered, slabs], in_specs=[SM] * 2 + [AN] + [VM] * 8, out_specs=[VM] * 5,
        scratch_shapes=[dma((4,))], input_output_aliases={10: 4},
        compiler_params=params(8), cost_estimate=COST, name="near1",
    )(*meta, intersection, exch, energy, vmem(x0), vmem(i0a), vmem(i0b), *swap(i0a, i0b), vmem(inter))
    inter = vmem(inter)
    x1, acc, amps = pl.pallas_call(
        across_kernel, out_shape=[tiles4, tiles8, tiles8],
        in_specs=[SM] * 2 + [VM] * 5, out_specs=[VM] * 3, input_output_aliases={5: 1, 6: 2},
        compiler_params=params(8), cost_estimate=COST, name="across",
    )(*meta, inter, vmem(xh), vmem(recip), vmem(acc), vmem(amps))
    xh1 = lax.ppermute(x1, "row", other_chip)
    i1a, i1b, acc, amps, recip = pl.pallas_call(
        rest_kernel, out_shape=[tiles2, tiles2] + [tiles8] * 3,
        in_specs=[SM] * 2 + [VM] * 8, out_specs=[VM] * 5, input_output_aliases={7: 2, 8: 3, 9: 4},
        compiler_params=params(8), cost_estimate=COST, name="rest",
    )(*meta, inter, exch, energy, vmem(src), vmem(xh), vmem(acc), vmem(amps), vmem(recip))
    acc, sq = pl.pallas_call(
        near_kernel_2, out_shape=[tiles8, pltpu.VMEM((8, 128), F32)], in_specs=[SM] * 2 + [VM] * 10, out_specs=[VM] * 2,
        scratch_shapes=[gathered], input_output_aliases={11: 0},
        compiler_params=params(8), cost_estimate=COST, name="near2",
    )(*meta, inter, exch, energy, vmem(x1), vmem(i1a), vmem(i1b), *swap(i1a, i1b), vmem(amps), vmem(acc))
    sums, acc = pl.pallas_call(
        last_kernel, out_shape=[pltpu.VMEM((2 * count, 128), F32), tiles8],
        in_specs=[SM] * 2 + [VM] * 4, out_specs=[VM, VM], input_output_aliases={5: 1},
        compiler_params=params(8), cost_estimate=COST, name="last",
    )(*meta, inter, vmem(xh1), vmem(sq), vmem(acc))
    out = pl.pallas_call(
        output_kernel, out_shape=jax.ShapeDtypeStruct((8, v, v), F32), in_specs=[SM] + [VM] * 3, out_specs=AN,
        scratch_shapes=[pltpu.VMEM((8, v, v), F32), dma((8,))],
        compiler_params=params(16), name="output",
        cost_estimate=pl.CostEstimate(flops=10**7, bytes_accessed=10**7, transcendentals=0),
    )(lists, vmem(recip), vmem(amps), vmem(acc))
    sums = lax.all_to_all(sums, "row", 0, 0, tiled=True)
    norms = jnp.sqrt(jnp.sum(sums.reshape(count, 2, 128), axis=(0, 2)) / (amp_exch.shape[0] * count * v * v))
    return out, norms


def solution(mesh):
    whole = P(("grp", "row"))
    return jax.shard_map(
        on_device, mesh=mesh, in_specs=(whole,) * 8, out_specs=(whole, P("grp")), check_vma=False
    )
```

```python
import functools

import jax
import jax.numpy as jnp
from jax import lax
from jax.experimental import pallas as pl
from jax.experimental.pallas import tpu as pltpu
from jax.sharding import PartitionSpec as P

F32 = jnp.float32
BF16 = jnp.bfloat16
VM = pl.BlockSpec(memory_space=pltpu.VMEM)
SM = pl.BlockSpec(memory_space=pltpu.SMEM)
AN = pl.BlockSpec(memory_space=pl.ANY)
CAP = 72
LONG, SHORT = 24, 8
COUNTS, LIVE = 4 * CAP, 4 * CAP + 4
GAP = 4 * CAP
MIB = 1 << 20


def base_slot():
    return lax.rem(lax.axis_index("row"), 2) * 4


def slots_of(first, end):
    base = base_slot()
    return [(q + base) & 7 for q in range(first, end)]


def params(mib, **kw):
    return pltpu.CompilerParams(vmem_limit_bytes=mib * MIB, **kw)


COST = pl.CostEstimate(flops=1000, bytes_accessed=1000, transcendentals=0)


def vmem(x):
    return pltpu.with_memory_space_constraint(x, pltpu.VMEM)


def hbm(x):
    return pltpu.with_memory_space_constraint(x, pltpu.HBM)


def denominators(energy, gaps, slots):
    rows = [energy[pl.ds(p, 1), :] for p in slots]
    fill = [jnp.zeros_like(rows[0])] * (8 - len(rows))
    cols = jnp.transpose(jnp.concatenate(rows + fill, axis=0))
    return [cols[:, i : i + 1] + rows[i] + gaps[i] for i in range(len(slots))]


def start_all(pairs, sems):
    copies = [pltpu.make_async_copy(a, b, sems.at[i]) for i, (a, b) in enumerate(pairs)]
    for c in copies:
        c.start()
    return copies


def first_kernel(exch, energy, gap, live, out, buf, en, gp, lv, sem, sems):
    slots = slots_of(0, 4)
    small = start_all([(energy, en), (gap, gp), (live, lv)], sems)
    tiles = start_all([(exch.at[p], buf.at[i]) for i, p in enumerate(slots)], sem)
    for c in small:
        c.wait()
    dens = denominators(en, [gp[p] for p in slots], slots)
    factors = [-lv[p].astype(F32) / dens[i] for i, p in enumerate(slots)]
    for i in range(4):
        tiles[i].wait()
        out[i] = (buf[i].astype(F32) * factors[i]).astype(BF16)


def second_kernel(
    exch, energy, gap, live, fock, nslot, nlive, inter_hbm, x, out_a, out_b, ex, en, lists, coefs, inter,
    gp, lv, fk, ns, nl, table, ends, sem, sems, slab_sem,
):
    del x
    slots = slots_of(4, 8)
    base = base_slot()
    small = start_all([(energy, en), (gap, gp), (live, lv), (fock, fk), (nslot, ns), (nlive, nl)], sems)
    order = slots + slots_of(0, 4)
    tiles = start_all([(exch.at[p], ex.at[p]) for p in order], sem)
    slabs = start_all([(inter_hbm.at[p], inter.at[p]) for p in order[4:]], slab_sem)
    for c in small:
        c.wait()
    dens = denominators(en, [gp[p] for p in slots], slots)
    for i, p in enumerate(slots):
        tiles[i].wait()
        tile = (-lv[p].astype(F32) * ex[p].astype(F32) / dens[i]).astype(BF16)
        if i < 2:
            out_a[i] = tile
        else:
            out_b[i - 2] = tile

    for s in range(4):
        table[4 + s] = jnp.where(base == 0, (s << 9) | 3, ((8 + s) << 9) | 1)
        table[16 + s] = jnp.where(base == 0, ((8 + s) << 9) | 1, (s << 9) | 3)
    for s in range(8):
        table[8 + s] = (((s + base) & 7) << 9) | lv[s]
    for k in range(4):
        ends[k] = k * CAP

    def entry(i, _):
        q, n = i >> 3, i & 7
        p = (q + base) & 7
        what = table[ns[p, n]]
        which = (what & 2) + (q >> 2)
        pos = ends[which]
        lists[pos] = ((what >> 9) << 9) | (q << 6) | (p << 3) | n
        coefs[pos] = fk[p, n]
        ends[which] = pos + (nl[p, n] & lv[p] & what & 1)
        return 0

    lax.fori_loop(0, 64, entry, 0, unroll=4)
    for k in range(4):
        e = ends[k]
        lists[COUNTS + k] = e - k * CAP
        for u in range(LONG):
            lists[e + u] = base << 3
            coefs[e + u] = 0.0
    for p in range(8):
        lists[LIVE + p] = lv[p]
        coefs[GAP + p] = gp[p]
    for c in tiles[4:] + slabs:
        c.wait()


def step(at, size, lists, coefs, inter, src, acc):
    for u in range(size):
        code = lists[at + u]
        n, p, q, s = code & 7, (code >> 3) & 7, (code >> 6) & 7, code >> 9
        x = inter[p, n]
        h = jnp.dot(x, src[s], preferred_element_type=F32).astype(BF16)
        t = lax.dot_general(h, x, (((1,), (1,)), ((), ())), preferred_element_type=F32)
        acc[q] = acc[q] - coefs[at + u] * t


def steps(at, count, size, *refs):
    def body(i, _):
        step(at + i * size, size, *refs)
        return 0

    lax.fori_loop(0, count, body, 0)


def near_list(which, lists, *refs):
    at, count = which * CAP, lists[COUNTS + which]
    longs = (count + LONG - SHORT - 1) // LONG
    steps(at, longs, LONG, lists, *refs)
    left = jnp.maximum(count - longs * LONG + SHORT - 1, 0)
    steps(at + longs * LONG, left // SHORT, SHORT, lists, *refs)


def across_list_tail(which, lists, *refs):
    more = jnp.maximum(lists[COUNTS + which] - 1, 0) // SHORT
    steps(which * CAP + SHORT, more, SHORT, lists, *refs)


def gather(src, x, ia, ib, iha, ihb):
    src[0:4] = x[...]
    src[4:6] = ia[...]
    src[6:8] = ib[...]
    src[8:10] = iha[...]
    src[10:12] = ihb[...]


def start_half(half, lists, coefs, exch, energy, acc, amps, recip):
    slots = slots_of(4 * half, 4 * half + 4)
    dens = denominators(energy, [coefs[GAP + p] for p in slots], slots)
    for j, p in enumerate(slots):
        q = 4 * half + j
        ex = exch[p].astype(F32)
        a0 = -lists[LIVE + p].astype(F32) * ex / dens[j]
        amps[q] = a0
        recip[q] = 1.0 / dens[j]
        acc[q] = ex + dens[j] * a0


def update_half(half, lists, acc, amps, recip, out):
    each = 4 // len(out)
    for j, p in enumerate(slots_of(4 * half, 4 * half + 4)):
        q = 4 * half + j
        res = lists[LIVE + p].astype(F32) * acc[q]
        a1 = amps[q] - res * recip[q]
        amps[q] = a1
        out[j // each][j % each] = a1.astype(BF16)


def waits_longer():
    return ((lax.axis_index("row") + 1) & 2) != 0


def near_kernel_1(lists, coefs, inter_hbm, exch, energy, x, ia, ib, iha, ihb, inter_in, acc, amps, recip, src, inter, sem):
    del inter_in
    slabs = start_all([(inter_hbm.at[p], inter.at[p]) for p in slots_of(4, 8)], sem)
    gather(src, x, ia, ib, iha, ihb)
    start_half(0, lists, coefs, exch, energy, acc, amps, recip)
    near_list(0, lists, coefs, inter, src, acc)
    for c in slabs:
        c.wait()

    @pl.when(waits_longer())
    def _():
        start_half(1, lists, coefs, exch, energy, acc, amps, recip)
        near_list(1, lists, coefs, inter, src, acc)


def across_kernel(lists, coefs, inter, xh, recip, acc_in, amps_in, out, acc, amps):
    del acc_in, amps_in
    refs = (lists, coefs, inter, xh, acc)
    across_list_tail(2, *refs)
    step(2 * CAP, SHORT, *refs)
    update_half(0, lists, acc, amps, recip, [out])


def rest_kernel(lists, coefs, inter, exch, energy, src, xh, acc_in, amps_in, recip_in, out_a, out_b, acc, amps, recip):
    del acc_in, amps_in, recip_in

    @pl.when(jnp.logical_not(waits_longer()))
    def _():
        start_half(1, lists, coefs, exch, energy, acc, amps, recip)
        near_list(1, lists, coefs, inter, src, acc)

    refs = (lists, coefs, inter, xh, acc)
    across_list_tail(3, *refs)
    step(3 * CAP, SHORT, *refs)
    update_half(1, lists, acc, amps, recip, [out_a, out_b])


def squares(res):
    s = jnp.sum((res * res).reshape(32, 8, 256), axis=0)
    return s[:, :128] + s[:, 128:]


def near_kernel_2(lists, coefs, inter, exch, energy, x, ia, ib, iha, ihb, amps, acc_in, acc, sq, src):
    del acc_in
    slots = slots_of(0, 8)
    dens = denominators(energy, [coefs[GAP + p] for p in slots], slots)
    total = jnp.zeros((8, 128), F32)
    for q, p in enumerate(slots):
        total = total + squares(lists[LIVE + p].astype(F32) * acc[q])
        acc[q] = exch[p].astype(F32) + dens[q] * amps[q]
    sq[...] = total
    gather(src, x, ia, ib, iha, ihb)
    for half in range(2):
        near_list(half, lists, coefs, inter, src, acc)


def last_kernel(lists, coefs, inter, xh, sq1, acc_in, sums, acc):
    del acc_in
    total = jnp.zeros((8, 128), F32)
    slots = slots_of(0, 8)
    refs = (lists, coefs, inter, xh, acc)
    for half in range(2):
        across_list_tail(2 + half, *refs)
    for half in range(2):
        step((2 + half) * CAP, SHORT, *refs)
        for q in range(4 * half, 4 * half + 4):
            total = total + squares(lists[LIVE + slots[q]].astype(F32) * acc[q])
    row = lax.broadcasted_iota(jnp.int32, sums.shape, 0) & 1
    first = jnp.sum(sq1[...], axis=0, keepdims=True)
    sums[...] = jnp.where(row == 0, first, jnp.sum(total, axis=0, keepdims=True))


def output_kernel(lists, recip, amps, acc, out, buf, sem):
    copies = []
    for q, p in enumerate(slots_of(0, 8)):
        buf[q] = amps[q] - lists[LIVE + p].astype(F32) * acc[q] * recip[q]
        copies.append(pltpu.make_async_copy(buf.at[q], out.at[p], sem.at[q]))
        copies[-1].start()
    for c in copies:
        c.wait()


def on_device(amp_exch, pno_energy, pair_gap, fock, intersection, nbr_slot, nbr_live, pair_live):
    count = lax.axis_size("row")
    v = amp_exch.shape[-1]
    tiles4 = pltpu.VMEM((4, v, v), BF16)
    tiles8 = pltpu.VMEM((8, v, v), F32)
    dma = pltpu.SemaphoreType.DMA
    per_pair = [pltpu.SMEM((8,), F32), pltpu.SMEM((8,), jnp.int32)]
    same_chip = [(i, i ^ 1) for i in range(count) if (i ^ 1) < count]
    other_chip = [(i, i + 1) for i in range(1, count - 1, 2)]
    other_chip += [(j, i) for i, j in other_chip]
    big = [hbm(a) for a in (amp_exch, pno_energy, pair_gap, pair_live, fock, nbr_slot, nbr_live)]

    tiles2 = pltpu.VMEM((2, v, v), BF16)
    slabs = pltpu.VMEM(intersection.shape, BF16)
    intersection = hbm(intersection)
    x0 = pl.pallas_call(
        first_kernel, out_shape=tiles4, in_specs=[AN] * 4, out_specs=VM,
        scratch_shapes=[pltpu.VMEM((4, v, v), BF16), pltpu.VMEM((8, v), F32)] + per_pair + [dma((4,)), dma((3,))],
        compiler_params=params(8), cost_estimate=COST, name="first",
    )(*big[:4])
    xh = lax.ppermute(x0, "row", other_chip)
    i0a, i0b, exch, energy, lists, coefs, inter = pl.pallas_call(
        second_kernel,
        out_shape=[tiles2, tiles2, pltpu.VMEM((8, v, v), BF16), pltpu.VMEM((8, v), F32),
                   pltpu.SMEM((LIVE + 8,), jnp.int32), pltpu.SMEM((GAP + 8,), F32), slabs],
        in_specs=[AN] * 9, out_specs=[VM] * 4 + [SM] * 2 + [VM],
        scratch_shapes=per_pair + [pltpu.SMEM((8, 8), F32)] + [pltpu.SMEM((8, 8), jnp.int32)] * 2
        + [pltpu.SMEM((24,), jnp.int32), pltpu.SMEM((4,), jnp.int32), dma((8,)), dma((6,)), dma((4,))],
        compiler_params=params(8), cost_estimate=COST, name="second",
    )(*big, intersection, x0)

    def swap(*halves):
        return [vmem(lax.ppermute(h, "row", same_chip)) for h in halves]

    meta = (lists, coefs)
    exch, energy = vmem(exch), vmem(energy)
    gathered = pltpu.VMEM((12, v, v), BF16)
    acc, amps, recip, src, inter = pl.pallas_call(
        near_kernel_1, out_shape=[tiles8] * 3 + [gathered, slabs], in_specs=[SM] * 2 + [AN] + [VM] * 8, out_specs=[VM] * 5,
        scratch_shapes=[dma((4,))], input_output_aliases={10: 4},
        compiler_params=params(8), cost_estimate=COST, name="near1",
    )(*meta, intersection, exch, energy, vmem(x0), vmem(i0a), vmem(i0b), *swap(i0a, i0b), vmem(inter))
    inter = vmem(inter)
    x1, acc, amps = pl.pallas_call(
        across_kernel, out_shape=[tiles4, tiles8, tiles8],
        in_specs=[SM] * 2 + [VM] * 5, out_specs=[VM] * 3, input_output_aliases={5: 1, 6: 2},
        compiler_params=params(8), cost_estimate=COST, name="across",
    )(*meta, inter, vmem(xh), vmem(recip), vmem(acc), vmem(amps))
    xh1 = lax.ppermute(x1, "row", other_chip)
    i1a, i1b, acc, amps, recip = pl.pallas_call(
        rest_kernel, out_shape=[tiles2, tiles2] + [tiles8] * 3,
        in_specs=[SM] * 2 + [VM] * 8, out_specs=[VM] * 5, input_output_aliases={7: 2, 8: 3, 9: 4},
        compiler_params=params(8), cost_estimate=COST, name="rest",
    )(*meta, inter, exch, energy, vmem(src), vmem(xh), vmem(acc), vmem(amps), vmem(recip))
    acc, sq = pl.pallas_call(
        near_kernel_2, out_shape=[tiles8, pltpu.VMEM((8, 128), F32)], in_specs=[SM] * 2 + [VM] * 10, out_specs=[VM] * 2,
        scratch_shapes=[gathered], input_output_aliases={11: 0},
        compiler_params=params(8), cost_estimate=COST, name="near2",
    )(*meta, inter, exch, energy, vmem(x1), vmem(i1a), vmem(i1b), *swap(i1a, i1b), vmem(amps), vmem(acc))
    sums, acc = pl.pallas_call(
        last_kernel, out_shape=[pltpu.VMEM((2 * count, 128), F32), tiles8],
        in_specs=[SM] * 2 + [VM] * 4, out_specs=[VM, VM], input_output_aliases={5: 1},
        compiler_params=params(8), cost_estimate=COST, name="last",
    )(*meta, inter, vmem(xh1), vmem(sq), vmem(acc))
    out = pl.pallas_call(
        output_kernel, out_shape=jax.ShapeDtypeStruct((8, v, v), F32), in_specs=[SM] + [VM] * 3, out_specs=AN,
        scratch_shapes=[pltpu.VMEM((8, v, v), F32), dma((8,))],
        compiler_params=params(16), name="output",
        cost_estimate=pl.CostEstimate(flops=10**7, bytes_accessed=10**7, transcendentals=0),
    )(lists, vmem(recip), vmem(amps), vmem(acc))
    sums = lax.all_to_all(sums, "row", 0, 0, tiled=True)
    norms = jnp.sqrt(jnp.sum(sums.reshape(count, 2, 128), axis=(0, 2)) / (amp_exch.shape[0] * count * v * v))
    return out, norms


def solution(mesh):
    whole = P(("grp", "row"))
    return jax.shard_map(
        on_device, mesh=mesh, in_specs=(whole,) * 8, out_specs=(whole, P("grp")), check_vma=False
    )
```
